32 devices in a mesh: expert: 8 (over z, y), tensor: 4 (over x, core).
Axes of the slice: x: 2, y: 2, z: 4, core: 2. Of those that a mesh axis runs over, the one named last changes fastest.
Arguments:
- block_input: bfloat16 [4096, 768], P('expert'), may hold values from -6 to 6
- cotangent: bfloat16 [4096, 768], P('expert'), may hold values from -6 to 6
- lengths: int32 [8], P('expert'), may hold values from 1 to 512, 3072 in all
- routes: int32 [4096, 1], P('expert'), may hold values from 0 to 7; in each aligned block of 512 rows (0 to 511, 512 to 1023, ...) at most 72 rows name the same one
- norm_gains: float32 [2, 768], replicated, may hold values from 0.5 to 1.5
- gains_mean: float32 [2, 768], replicated, may hold values from -56 to 56
- gains_square: float32 [2, 768], replicated, may hold values from 8.192 to 32.768
- position_bias: float32 [32, 12], replicated, may hold values from -3 to 3
- bias_mean: float32 [32, 12], replicated, may hold values from -40 to 40
- bias_square: float32 [32, 12], replicated, may hold values from 4.096 to 16.384
- router: float32 [768, 2], replicated, may hold values from -0.15625 to 0.15625
- router_mean: float32 [768, 2], replicated, may hold values from -640 to 640
- router_square: float32 [768, 2], replicated, may hold values from 1048.576 to 4194.304
- qkv_weight: float32 [3, 768, 768], P(None, 'expert', 'tensor'), may hold values from -0.21875 to 0.21875
- qkv_mean: float32 [3, 768, 768], P(None, 'expert', 'tensor'), may hold values from -40 to 40
- qkv_square: float32 [3, 768, 768], P(None, 'expert', 'tensor'), may hold values from 4.096 to 16.384
- out_weight: float32 [768, 768], P('tensor', 'expert'), may hold values from -3.5 to 3.5
- out_mean: float32 [768, 768], P('tensor', 'expert'), may hold values from -2.5 to 2.5
- out_square: float32 [768, 768], P('tensor', 'expert'), may hold values from 0.016 to 0.064
- expert_up: float32 [8, 768, 768], P('expert', 'tensor'), may hold values from -0.21875 to 0.21875
- up_mean: float32 [8, 768, 768], P('expert', 'tensor'), may hold values from -7 to 7
- up_square: float32 [8, 768, 768], P('expert', 'tensor'), may hold values from 0.128 to 0.512
- expert_down: float32 [8, 768, 768], P('expert', 'tensor'), may hold values from -0.21875 to 0.21875
- down_mean: float32 [8, 768, 768], P('expert', 'tensor'), may hold values from -10 to 10
- down_square: float32 [8, 768, 768], P('expert', 'tensor'), may hold values from 0.256 to 1.024
Outputs:
- block_output: bfloat16 [4096, 768], P(('expert', 'tensor'))
- input_grad: float32 [4096, 768], P(('expert', 'tensor'))
- new_gains_mean: float32 [2, 768], replicated
- new_gains_square: float32 [2, 768], replicated
- new_norm_gains: float32 [2, 768], replicated
- new_bias_mean: float32 [32, 12], replicated
- new_bias_square: float32 [32, 12], replicated
- new_position_bias: float32 [32, 12], replicated
- new_router_mean: float32 [768, 2], replicated
- new_router_square: float32 [768, 2], replicated
- new_router: float32 [768, 2], replicated
- new_qkv_mean: float32 [3, 768, 768], P(None, 'expert', 'tensor')
- new_qkv_square: float32 [3, 768, 768], P(None, 'expert', 'tensor')
- new_qkv_weight: float32 [3, 768, 768], P(None, 'expert', 'tensor')
- new_out_mean: float32 [768, 768], P('tensor', 'expert')
- new_out_square: float32 [768, 768], P('tensor', 'expert')
- new_out_weight: float32 [768, 768], P('tensor', 'expert')
- new_up_mean: float32 [8, 768, 768], P('expert', 'tensor')
- new_up_square: float32 [8, 768, 768], P('expert', 'tensor')
- new_expert_up: float32 [8, 768, 768], P('expert', 'tensor')
- new_down_mean: float32 [8, 768, 768], P('expert', 'tensor')
- new_down_square: float32 [8, 768, 768], P('expert', 'tensor')
- new_expert_down: float32 [8, 768, 768], P('expert', 'tensor')
The draws below stay inside these ranges and needn't reach their ends.
Inputs may be any that keep to these rules, and one draw needn't show every extreme that they name: Replica routes[t] serves token t and belongs to expert routes[t] // 4. Among the 512 rows of one index of the expert axis no replica is named by more than 72 rows, a bound that some block reaches. lengths[s] is the number of live tokens at the head of sequence s; some sequence has all 512.
All inputs are finite; a program needn't handle non-finite values. No bound on the sum of `lengths` on one device may be relied on, other than what follows from the above.
Results may differ from the reference program's by a relative error of at most 0.015.
Values may be sent and summed in bfloat16 or wider, within the bound.
No kernel may reach another device: no remote copies, remote signals or barrier semaphores. Data moves between devices by JAX's collectives and lax.ppermute only.
A program may use at most 128 MiB of HBM per device.

```python
import math
import jax
import jax.numpy as jnp
import numpy as np
from jax import lax

D = 768
HEADS = 12
HEAD_DIM = 64
FF = 3072
BUCKETS = 32
MAX_DIST = 128
GROUP = 4
STEP = 10
SEQ_LEN = 512
EXPERTS = 2
CAP = 72
TOKENS = 4096
FF_Q = 768
FAN_O = 3
FAN_X = 768
N_EXPERT = 8


def block_levels(stream_key, shape, pieces, smallest, largest):
    level, own = 1.0, jax.random.fold_in(stream_key, 6)
    for axis_at, blocks in pieces:
        steps = jnp.exp(jax.random.uniform(jax.random.fold_in(own, axis_at), (blocks,), jnp.float32, smallest / len(pieces), largest / len(pieces)))
        level = level * jnp.repeat(steps, shape[axis_at] // blocks).reshape([-1 if axis == axis_at else 1 for axis in range(len(shape))])
    return level


def split_up(amount, total, most, skew):
    portions = [(1 << 20) // math.isqrt(rank ** skew) + 1 for rank in range(2, amount + 1)]
    rest, holding = total - most - (amount - 1), [1] * (amount - 1)
    while rest > 0:
        free = [i for i in range(amount - 1) if holding[i] < most]
        whole, budget = sum([portions[i] for i in free]), rest
        for i in free:
            more = min(most - holding[i], max(1, budget * portions[i] // whole), rest)
            holding[i] = holding[i] + more
            rest = rest - more
    return np.array([most] + holding)


def uneven(own_key, number_of, total, bound, skew):
    if number_of == 2:
        one = jax.random.randint(own_key, (), max(1, total - bound), min(bound, total - 1) + 1)
        return jnp.stack([one, total - one])
    sizes = jnp.asarray(split_up(number_of, total, bound, skew), jnp.int32)
    twos = (number_of - 1) // 2
    donor, taker = sizes[1:1 + 2 * twos:2], sizes[2:2 + 2 * twos:2]
    slack = jnp.minimum(donor - 1, bound - taker)
    moved = jax.random.randint(jax.random.fold_in(own_key, 1), (twos,), 0, 1 << 20) % (slack + 1)
    sizes = sizes.at[1:1 + 2 * twos:2].set(donor - moved).at[2:2 + 2 * twos:2].set(taker + moved)
    return sizes[jax.random.permutation(jax.random.fold_in(own_key, 2), number_of)]


def routed_block(own_key, own, number, rows, count, top, most, lean):
    order = jax.random.permutation(own_key, count)
    crowded, ordinary = portions_of(count, rows * top, most, lean, True), portions_of(count, rows * top, most, lean, False)
    places = jnp.arange(count)

    def named(tallies, offset_by):
        used = int((tallies > 0).sum())
        fixed = max(1, used // 4)
        shifted = fixed + (places - fixed + offset_by * (used - fixed)) % max(1, count - fixed)
        return jnp.zeros((count,), jnp.int32).at[order[jnp.where(places < fixed, places, shifted)]].set(jnp.asarray(tallies, jnp.int32))

    tallies = jnp.where(number % 4 == 0, named(crowded, number // 4), named(ordinary, number - number // 4 - 1))
    mixed = jax.random.permutation(jax.random.fold_in(own, 3), count)
    giver, sink = mixed[0:count // 2 * 2:2], mixed[1:count // 2 * 2:2]
    slack = jnp.minimum(tallies[giver] - 1, most - tallies[sink]) // 2
    slack = jnp.where((giver == order[0]) | (sink == order[0]) | (tallies[sink] == 0), 0, jnp.maximum(slack, 0))
    shifted = jax.random.randint(jax.random.fold_in(own, 4), (count // 2,), 0, 1 << 20) % (slack + 1)
    tallies = tallies.at[giver].add(-shifted).at[sink].add(shifted)
    labels = jnp.searchsorted(jnp.cumsum(tallies), jnp.arange(rows * top), side="right").astype(jnp.int32)
    table = labels.reshape(top, rows).T
    table = table[jax.random.permutation(jax.random.fold_in(own, 1), rows)]
    offset_by = jax.random.randint(jax.random.fold_in(own, 2), (rows, 1), 0, top)
    return jnp.take_along_axis(table, (jnp.arange(top)[None, :] + offset_by) % top, axis=1)


def portions_of(count, total, most, slope, full):
    weights = [(1 << 20) // math.isqrt(rank ** slope) + 1 for rank in range(1, count + 1)]
    largest = most if full else min(most, max(-(-total // count), total * weights[0] // sum(weights)))
    least = 1 if total - largest >= count - 1 else 0
    holding, spare = [largest] + [least] * (count - 1), total - largest - least * (count - 1)
    while spare > 0:
        movable = [i for i in range(1, count) if holding[i] < largest] or [i for i in range(1, count) if holding[i] < most]
        mass, remaining = sum([weights[i] for i in movable]), spare
        for i in movable:
            addition = min(most - holding[i], max(1, remaining * weights[i] // mass), spare)
            holding[i] = holding[i] + addition
            spare = spare - addition
    return np.array(holding)


def normal_values(rng, shape, width, reach, pieces=(), kind=jnp.bfloat16):
    factor_of = block_levels(rng, shape, pieces, -0.22, 0.18) if pieces else 1.0
    values = jax.random.normal(rng, shape, jnp.float32) * width * factor_of
    return jnp.minimum(jnp.maximum(values, -reach), reach).astype(kind)


def setup_inputs(seed: int = 0) -> dict:
    key_of = jax.random.split(jax.random.key(seed), 26)
    block_input = normal_values(key_of[0], (TOKENS, D), 1.0, 6.0, ((0, 8),))
    cotangent = normal_values(key_of[1], (TOKENS, D), 1.0, 6.0, ((0, 8),))
    lengths = uneven(key_of[2], N_EXPERT, 3 * SEQ_LEN * N_EXPERT // 4, SEQ_LEN, 1).astype(jnp.int32)
    routes_keys = jax.random.split(jax.random.fold_in(key_of[3], 1), TOKENS // SEQ_LEN)
    routes_turns = jax.random.permutation(jax.random.fold_in(key_of[3], 3), TOKENS // SEQ_LEN)
    routes = jax.vmap(lambda own, number: routed_block(jax.random.fold_in(key_of[3], 2), own, number, SEQ_LEN, N_EXPERT, 1, CAP, 1))(routes_keys, routes_turns).reshape((TOKENS, 1))
    norm_gains = jnp.clip(1.0 + 0.1 * jax.random.normal(key_of[4], (2, D), jnp.float32), 0.5, 1.5)
    gains_mean = normal_values(key_of[5], (2, D), (0.1 * (2 * TOKENS) ** 0.5), 56.0, (), jnp.float32)
    gains_square = jnp.clip(jnp.exp(jax.random.uniform(key_of[6], (2, D), jnp.float32, math.log(8.192), math.log(32.768))), 8.192, 32.768)
    position_bias = normal_values(key_of[7], (BUCKETS, HEADS), 0.5, 3.0, (), jnp.float32)
    bias_mean = normal_values(key_of[8], (BUCKETS, HEADS), (0.1 * (64 * D * N_EXPERT // (FAN_O * BUCKETS)) ** 0.5), 40.0, (), jnp.float32)
    bias_square = jnp.clip(jnp.exp(jax.random.uniform(key_of[9], (BUCKETS, HEADS), jnp.float32, math.log(4.096), math.log(16.384))), 4.096, 16.384)
    router = normal_values(key_of[10], (D, EXPERTS), (2 * D) ** -0.5, 0.15625, (), jnp.float32)
    router_mean = normal_values(key_of[11], (D, EXPERTS), (0.1 * max(1, (D * FF // FAN_X) * TOKENS // (3 * EXPERTS * EXPERTS)) ** 0.5), 640.0, (), jnp.float32)
    router_square = jnp.clip(jnp.exp(jax.random.uniform(key_of[12], (D, EXPERTS), jnp.float32, math.log(1048.576), math.log(4194.304))), 1048.576, 4194.304)
    qkv_weight = normal_values(key_of[13], (3, D, D), D ** -0.5, 0.21875, ((1, 8), (2, 4)), jnp.float32)
    qkv_mean = normal_values(key_of[14], (3, D, D), (0.1 * (2 * D * N_EXPERT // FAN_O) ** 0.5), 40.0, ((1, 8), (2, 4)), jnp.float32)
    qkv_square = jnp.clip(jnp.exp(math.log(16.384) - 1.3862944 * jax.random.uniform(key_of[15], (3, D, D), jnp.float32) ** block_levels(key_of[15], (3, D, D), ((1, 8), (2, 4)), -0.2, 0.2)), 4.096, 16.384)
    out_weight = normal_values(key_of[16], (D, D), FAN_O ** -0.5, 3.5, ((0, 4), (1, 8)), jnp.float32)
    out_mean = normal_values(key_of[17], (D, D), (0.1 * (2 * N_EXPERT) ** 0.5), 2.5, ((0, 4), (1, 8)), jnp.float32)
    out_square = jnp.clip(jnp.exp(math.log(0.064) - 1.3862944 * jax.random.uniform(key_of[18], (D, D), jnp.float32) ** block_levels(key_of[18], (D, D), ((0, 4), (1, 8)), -0.2, 0.2)), 0.016, 0.064)
    expert_up = normal_values(key_of[19], (N_EXPERT, FF_Q, D), D ** -0.5, 0.21875, ((0, 8), (1, 4)), jnp.float32)
    up_mean = normal_values(key_of[20], (N_EXPERT, FF_Q, D), (0.1 * max(1, D * SEQ_LEN // FAN_X // (EXPERTS * EXPERTS)) ** 0.5), 7.0, ((0, 8), (1, 4)), jnp.float32)
    up_square = jnp.clip(jnp.exp(math.log(0.512) - 1.3862944 * jax.random.uniform(key_of[21], (N_EXPERT, FF_Q, D), jnp.float32) ** block_levels(key_of[21], (N_EXPERT, FF_Q, D), ((0, 8), (1, 4)), -0.2, 0.2)), 0.128, 0.512)
    expert_down = normal_values(key_of[22], (N_EXPERT, FF_Q, D), FAN_X ** -0.5, 0.21875, ((0, 8), (1, 4)), jnp.float32)
    down_mean = normal_values(key_of[23], (N_EXPERT, FF_Q, D), (0.1 * max(1, 2 * SEQ_LEN // (EXPERTS * EXPERTS)) ** 0.5), 10.0, ((0, 8), (1, 4)), jnp.float32)
    down_square = jnp.clip(jnp.exp(math.log(1.024) - 1.3862944 * jax.random.uniform(key_of[24], (N_EXPERT, FF_Q, D), jnp.float32) ** block_levels(key_of[24], (N_EXPERT, FF_Q, D), ((0, 8), (1, 4)), -0.2, 0.2)), 0.256, 1.024)
    return {"block_input": block_input, "cotangent": cotangent, "lengths": lengths, "routes": routes, "norm_gains": norm_gains, "gains_mean": gains_mean, "gains_square": gains_square, "position_bias": position_bias, "bias_mean": bias_mean, "bias_square": bias_square, "router": router, "router_mean": router_mean, "router_square": router_square, "qkv_weight": qkv_weight, "qkv_mean": qkv_mean, "qkv_square": qkv_square, "out_weight": out_weight, "out_mean": out_mean, "out_square": out_square, "expert_up": expert_up, "up_mean": up_mean, "up_square": up_square, "expert_down": expert_down, "down_mean": down_mean, "down_square": down_square}


@jax.custom_vjp
def low(v):
    return lax.optimization_barrier(v.astype(jnp.bfloat16)).astype(jnp.float32)

@jax.custom_vjp
def low_back(v):
    return v

def low_keep(v):
    return (low(v), None)

def low_pass(kept, grad):
    return (grad,)

def back_keep(v):
    return (v, None)

def back_low(kept, grad):
    return (low(grad),)
low.defvjp(low_keep, low_pass)
low_back.defvjp(back_keep, back_low)
EPS_NORM = 1e-06
BETA_ONE = 0.9
BETA_TWO = 0.999
EPS_ADAM = 1e-08
DECAY = 0.01
MASKED = -1e+30
HIGH = lax.Precision.HIGHEST

def bucket_of(offset):
    half = BUCKETS // 2
    exact = half // 2
    sign_part = jnp.where(offset > 0, half, 0).astype(jnp.int32)
    distance = jnp.abs(offset).astype(jnp.int32)
    far = jnp.full(offset.shape, exact, jnp.int32)
    for level in range(exact + 1, half):
        limit = int(np.ceil(exact * (MAX_DIST / exact) ** ((level - exact) / (half - exact)) - 1e-09))
        far = far + (distance >= limit).astype(jnp.int32)
    return sign_part + jnp.where(distance < exact, distance, far)

def rms_norm(values, gain):
    scale = lax.rsqrt(lax.optimization_barrier(jnp.mean(values * values, axis=-1, keepdims=True)) + EPS_NORM)
    return values * scale * gain

def attend(normed, length, weights, table):
    hidden = jnp.einsum('ld,cdw->clw', normed, weights, precision=HIGH)
    hidden = low_back(low(hidden))
    heads = hidden.reshape(3, SEQ_LEN, HEADS, HEAD_DIM).transpose(0, 2, 1, 3)
    queries = heads[0]
    keys = heads[1]
    values = heads[2]
    scores = jnp.einsum('hqd,hkd->hqk', queries, keys, precision=HIGH) * HEAD_DIM ** (-0.5)
    position = jnp.arange(SEQ_LEN, dtype=jnp.int32)
    buckets = bucket_of(position[None, :] - position[:, None])
    scores = low_back(scores + jnp.take(table.T, buckets, axis=1))
    scores = jnp.where(position[None, None, :] < length, scores, MASKED)
    probs = low(jax.nn.softmax(scores, axis=-1))
    mixed = jnp.einsum('hqk,hkd->hqd', probs, values, precision=HIGH)
    return low_back(low(mixed.transpose(1, 0, 2).reshape(SEQ_LEN, D)))

def expert_step(operands):
    rows, weight_in, weight_out = operands
    pre = low_back(jnp.dot(rows, weight_in.T, precision=HIGH))
    act = low(jax.nn.gelu(pre, approximate=True))
    return jnp.dot(act, weight_out, precision=HIGH)

def forward(hidden, gains, table, gate_weight, qkv, out_w, weight_in, weight_out, lengths, routes):
    normed = low(rms_norm(hidden, gains[0]))
    qkv_low = low(qkv)

    def one_sequence(operands):
        return attend(operands[0], operands[1], qkv_low, table)
    mixed = lax.map(jax.checkpoint(one_sequence), (normed.reshape(N_EXPERT, SEQ_LEN, D), lengths))
    branch = low_back(jnp.dot(mixed.reshape(TOKENS, D), low(out_w), precision=HIGH))
    middle = hidden + branch
    normed_two = low(rms_norm(middle, gains[1]))
    probs = jax.nn.softmax(jnp.dot(normed_two, gate_weight, precision=HIGH), axis=-1)
    group = (routes[:, 0] // GROUP).astype(jnp.int32)
    chosen = group[:, None] == jnp.arange(EXPERTS, dtype=jnp.int32)[None, :]
    gate = lax.optimization_barrier(jnp.sum(jnp.where(chosen, probs, 0.0), axis=-1))
    ranks = jnp.cumsum(chosen.astype(jnp.int32), axis=0) - 1
    max_rows = GROUP * N_EXPERT * CAP
    place = (group * max_rows + lax.optimization_barrier(jnp.sum(jnp.where(chosen, ranks, 0), axis=-1))).astype(jnp.int32)
    buffer = jnp.zeros((EXPERTS * max_rows, D), normed_two.dtype).at[place].set(normed_two)
    results = lax.map(jax.checkpoint(expert_step), (buffer.reshape(EXPERTS, max_rows, D), low(weight_in).reshape(EXPERTS, FF, D), low(weight_out).reshape(EXPERTS, FF, D)))
    expert_out = low_back(results.reshape(EXPERTS * max_rows, D)[place])
    return middle + gate[:, None] * expert_out

def adamw(weight, mean, square, grad, rate, decay):
    mean_new = BETA_ONE * mean + (1.0 - BETA_ONE) * grad
    square_new = BETA_TWO * square + (1.0 - BETA_TWO) * grad * grad
    mean_hat = mean_new / (1.0 - BETA_ONE ** STEP)
    square_hat = square_new / (1.0 - BETA_TWO ** STEP)
    weight_new = weight - rate * (mean_hat / (jnp.sqrt(square_hat) + EPS_ADAM) + decay * weight)
    return (mean_new, square_new, weight_new)

def reference(block_input, cotangent, lengths, routes, norm_gains, gains_mean, gains_square, position_bias, bias_mean, bias_square, router, router_mean, router_square, qkv_weight, qkv_mean, qkv_square, out_weight, out_mean, out_square, expert_up, up_mean, up_square, expert_down, down_mean, down_square):

    def wrapped(hidden, gains, table, gate_weight, qkv, out_w, weight_in, weight_out):
        return forward(hidden, gains, table, gate_weight, qkv, out_w, weight_in, weight_out, lengths, routes)
    primals = (block_input.astype(jnp.float32), norm_gains, position_bias, router, qkv_weight, out_weight, expert_up, expert_down)
    result, pullback = jax.vjp(wrapped, *primals)
    grads = pullback(cotangent.astype(jnp.float32))
    new_gains_mean, new_gains_square, new_norm_gains = adamw(norm_gains, gains_mean, gains_square, grads[1], 0.3, 0.0)
    new_bias_mean, new_bias_square, new_position_bias = adamw(position_bias, bias_mean, bias_square, grads[2], 1.5, 0.0)
    new_router_mean, new_router_square, new_router = adamw(router, router_mean, router_square, grads[3], 3.0 * (2 * D) ** (-0.5), DECAY)
    new_qkv_mean, new_qkv_square, new_qkv_weight = adamw(qkv_weight, qkv_mean, qkv_square, grads[4], 3.0 * D ** (-0.5), DECAY)
    new_out_mean, new_out_square, new_out_weight = adamw(out_weight, out_mean, out_square, grads[5], 3.0 * FAN_O ** (-0.5), DECAY)
    new_up_mean, new_up_square, new_expert_up = adamw(expert_up, up_mean, up_square, grads[6], 3.0 * D ** (-0.5), DECAY)
    new_down_mean, new_down_square, new_expert_down = adamw(expert_down, down_mean, down_square, grads[7], 3.0 * FAN_X ** (-0.5), DECAY)
    return (result.astype(jnp.bfloat16), grads[0], new_gains_mean, new_gains_square, new_norm_gains, new_bias_mean, new_bias_square, new_position_bias, new_router_mean, new_router_square, new_router, new_qkv_mean, new_qkv_square, new_qkv_weight, new_out_mean, new_out_square, new_out_weight, new_up_mean, new_up_square, new_expert_up, new_down_mean, new_down_square, new_expert_down)
```

```python
import functools

import jax
import jax.numpy as jnp
import numpy as np
from jax import lax
from jax.experimental import pallas as pl
from jax.experimental.pallas import tpu as pltpu
from jax.sharding import PartitionSpec as P

D = 768
HEADS = 12
HEAD_DIM = 64
FF = 3072
BUCKETS = 32
MAX_DIST = 128
GROUP = 4
STEP = 10
SEQ_LEN = 512
FAN_O = 3


EPS_NORM = 1e-06
BETA_ONE = 0.9
BETA_TWO = 0.999
EPS_ADAM = 1e-08
DECAY = 0.01
MASKED = -1e30
HIGH = lax.Precision.HIGHEST
LOW = jnp.bfloat16
WIDE = jnp.float32


def swap(block, axis, distance):
    count = lax.axis_size(axis)
    return lax.ppermute(block, axis, [(low, low ^ distance) for low in range(count)])


def exchange(pieces):
    count = len(pieces)
    if count <= 8:
        return [pieces[0]] + [swap(pieces[m], "expert", m) for m in range(1, count)]
    order = lax.axis_index("expert") ^ jnp.arange(count, dtype=jnp.int32)
    sent = jnp.take(jnp.stack(pieces), order, axis=0)
    came = lax.all_to_all(sent, "expert", split_axis=0, concat_axis=0, tiled=True)
    came = jnp.take(came, order, axis=0)
    return [came[m] for m in range(count)]


def tensor_blocks(block):
    far = swap(block, "tensor", 2)
    near = swap(block, "tensor", 1)
    return [block, near, far, swap(far, "tensor", 1)]


def bucket_of(offset):
    half = BUCKETS // 2
    exact = half // 2
    distance = np.abs(offset)
    far = np.full(offset.shape, exact, np.int32)
    for level in range(exact + 1, half):
        limit = int(
            np.ceil(exact * (MAX_DIST / exact) ** ((level - exact) / (half - exact)) - 1e-09)
        )
        far = far + (distance >= limit)
    return np.where(offset > 0, half, 0) + np.where(distance < exact, distance, far)


def offset_hits(offsets, width):
    hits = (bucket_of(offsets)[:, None] == np.arange(width)[None, :]) & (
        np.abs(offsets)[:, None] < SEQ_LEN
    )
    return hits.astype(np.float32)


def adamw(weight, mean, square, grad, rate, decay):
    mean_new = BETA_ONE * mean + (1.0 - BETA_ONE) * grad
    square_new = BETA_TWO * square + (1.0 - BETA_TWO) * grad * grad
    mean_hat = mean_new / (1.0 - BETA_ONE**STEP)
    square_hat = square_new / (1.0 - BETA_TWO**STEP)
    weight_new = weight - rate * (mean_hat / (jnp.sqrt(square_hat) + EPS_ADAM) + decay * weight)
    return (mean_new, square_new, weight_new)


def dot_rows(left, right):
    return lax.dot_general(left, right, (((0,), (0,)), ((), ())), preferred_element_type=WIDE)


def dot_cols(left, right):
    return lax.dot_general(left, right, (((1,), (1,)), ((), ())), preferred_element_type=WIDE)


def dot_plain(left, right):
    return jnp.dot(left, right, preferred_element_type=WIDE)


def call(kernel, outs, operands, scalars=0, scratch=()):
    whole = pl.BlockSpec(memory_space=pltpu.VMEM)
    return pl.pallas_call(
        kernel,
        out_shape=outs,
        in_specs=[pl.BlockSpec(memory_space=pltpu.SMEM)] * scalars
        + [whole] * (len(operands) - scalars),
        out_specs=[whole] * len(outs),
        scratch_shapes=list(scratch),
        compiler_params=pltpu.CompilerParams(vmem_limit_bytes=48 * 2**20),
    )(*operands)


def shape_of(dtype, *sizes):
    return jax.ShapeDtypeStruct(sizes, dtype)


def head_masks(width):
    lane = lax.broadcasted_iota(jnp.int32, (1, width), 1)
    return [
        (lane >= h * HEAD_DIM) & (lane < (h + 1) * HEAD_DIM) for h in range(width // HEAD_DIM)
    ]


def slot_hits(slot_row, count):
    slots = lax.broadcasted_iota(jnp.int32, (count, slot_row.shape[1]), 0)
    return jnp.where(slots == slot_row, 1.0, 0.0).astype(LOW)


def prepare_kernel(x_ref, cot_ref, gain_ref, slot_ref, offset_ref, n_ref, bias_ref, xs_ref, cs_ref):
    values = x_ref[...].astype(WIDE)
    scale = lax.rsqrt(jnp.mean(values * values, axis=-1, keepdims=True) + EPS_NORM)
    n_ref[...] = (values * scale * gain_ref[...]).astype(LOW)
    hits = slot_hits(slot_ref[...], xs_ref.shape[0])
    xs_ref[...] = dot_plain(hits, x_ref[...]).astype(LOW)
    cs_ref[...] = dot_plain(hits, cot_ref[...]).astype(LOW)
    for h in range(bias_ref.shape[0]):
        line = jnp.broadcast_to(offset_ref[h : h + 1, :], (SEQ_LEN, 2 * SEQ_LEN))
        turned = pltpu.roll(line, 0, 1, stride=1, stride_axis=0)
        bias_ref[h] = turned[:, :SEQ_LEN]


def forward_kernel(parts, *refs):
    place_ref, length_ref, n_ref, bias_ref, slot_ref = refs[:5]
    pieces = refs[5 : 5 + parts]
    w_ref, proj_ref, probs_ref = refs[5 + parts : 8 + parts]
    mixed_refs = refs[8 + parts : 12 + parts]
    width = mixed_refs[0].shape[1]
    rows = D // parts
    if parts == 1:
        w_ref[...] = pieces[0][...]
    else:
        for m in range(parts):
            at = pl.multiple_of((place_ref[0] ^ m) * rows, rows)
            w_ref[pl.ds(at, rows), :] = pieces[m][...]
    proj_ref[...] = dot_plain(n_ref[...], w_ref[:, : 3 * width]).astype(LOW)
    query = proj_ref[:, :width]
    key = proj_ref[:, width : 2 * width]
    value = proj_ref[:, 2 * width : 3 * width]
    live = lax.broadcasted_iota(jnp.int32, (1, SEQ_LEN), 1) < length_ref[0]
    mixed = jnp.zeros((SEQ_LEN, width), WIDE)
    for h, mask in enumerate(head_masks(width)):
        picked = query * jnp.where(mask, 1.0, 0.0).astype(LOW)
        scores = dot_cols(picked, key) * HEAD_DIM ** (-0.5) + bias_ref[h]
        scores = jnp.where(live, scores, MASKED)
        expo = jnp.exp(scores - jnp.max(scores, axis=-1, keepdims=True))
        probs = expo * (1.0 / jnp.sum(expo, axis=-1, keepdims=True))
        probs_ref[h] = probs
        mixed = jnp.where(mask, dot_plain(probs.astype(LOW), value), mixed)
    count = mixed_refs[0].shape[0]
    hits = slot_hits(slot_ref[...], 4 * count)
    slots = dot_plain(hits, mixed.astype(LOW)).astype(LOW)
    for m in range(4):
        mixed_refs[m][...] = slots[m * count : (m + 1) * count, :]


def pick_hits(rows, share, m):
    row = lax.broadcasted_iota(jnp.int32, (rows, share), 0)
    col = lax.broadcasted_iota(jnp.int32, (rows, share), 1)
    return jnp.where(row == col + m * share, 1.0, 0.0).astype(LOW)


def join_shares(refs):
    share = refs[0].shape[0]
    rows = share * len(refs)
    total = dot_plain(pick_hits(rows, share, 0), refs[0][...])
    for m in range(1, len(refs)):
        total = total + dot_plain(pick_hits(rows, share, m), refs[m][...])
    return total


def cut_shares(rows, refs):
    for m in range(len(refs)):
        share = refs[m].shape[0]
        refs[m][...] = dot_rows(pick_hits(rows.shape[0], share, m), rows).astype(LOW)


def join_kernel(*refs):
    refs[-1][...] = join_shares(refs[:-1]).astype(LOW)


def route_probs(rows, router_ref):
    logits = lax.dot_general(
        rows.astype(WIDE),
        router_ref[...],
        (((1,), (1,)), ((), ())),
        precision=HIGH,
        preferred_element_type=WIDE,
    )
    expo = jnp.exp(logits - jnp.max(logits, axis=-1, keepdims=True))
    return expo / jnp.sum(expo, axis=-1, keepdims=True)


def middle_kernel(*refs):
    x_ref, gain_ref = refs[:2]
    mixed_refs, out_refs = refs[2:6], refs[6:10]
    middle_ref, normed_ref = refs[10:12]
    middle = x_ref[...].astype(WIDE)
    for m in range(4):
        middle = middle + dot_plain(mixed_refs[m][...], out_refs[m][...])
    middle_ref[...] = middle
    scale = lax.rsqrt(jnp.mean(middle * middle, axis=-1, keepdims=True) + EPS_NORM)
    normed = (middle * scale * gain_ref[...]).astype(LOW)
    normed_ref[...] = normed
    cut_shares(normed, refs[12:])


def expert_kernel(*refs):
    place_ref, router_ref = refs[:2]
    row_refs, cot_refs = refs[2:6], refs[6:10]
    up_refs, down_refs = refs[10:13], refs[13:16]
    rows_ref, grads_ref, act_ref, pre_grad_ref = refs[16:20]
    keep_ref, send_ref = refs[20:22]
    weight_up = jnp.concatenate([ref[...] for ref in up_refs], axis=0)
    near, far, pair = down_refs
    shard = near.shape[0]
    weight_down = jnp.concatenate([near[...], pair[:shard, :], far[...], pair[shard:, :]], axis=0)
    count = row_refs[0].shape[0]
    for at, m in enumerate((0, 2, 1, 3)):
        rows_ref[at * count : (at + 1) * count, :] = row_refs[m][...]
        grads_ref[at * count : (at + 1) * count, :] = cot_refs[m][...]
    rows = rows_ref[...]
    probs = route_probs(rows, router_ref)
    here = lax.broadcasted_iota(jnp.int32, (1, probs.shape[1]), 1) == place_ref[0] // GROUP
    gate = jnp.sum(jnp.where(here, probs, 0.0), axis=-1, keepdims=True)
    grads_ref[...] = (gate * grads_ref[...].astype(WIDE)).astype(LOW)
    pre = dot_cols(rows, weight_up)
    root = np.sqrt(2 / np.pi).astype(np.float32)
    bend = np.float32(0.044715)
    square = pre * pre
    curve = jnp.tanh(root * (pre + bend * square * pre))
    act_ref[...] = (0.5 * pre * (1.0 + curve)).astype(LOW)
    slope = 0.5 * (1.0 + curve) + 0.5 * pre * (1.0 - curve * curve) * root * (
        1.0 + 3.0 * bend * square
    )
    pre_grad_ref[...] = (slope * dot_cols(grads_ref[...], weight_down)).astype(LOW)
    out = dot_plain(act_ref[...], weight_down)
    back = dot_plain(pre_grad_ref[...], weight_up)
    keep_ref[:, :D] = out[: 2 * count]
    keep_ref[:, D:] = back[: 2 * count]
    send_ref[:, :D] = out[2 * count :].astype(LOW)
    send_ref[:, D:] = back[2 * count :].astype(LOW)


def expert_weights_kernel(rows_ref, grads_ref, act_ref, pre_grad_ref, *outs):
    up_keep_ref, up_send_ref, down_keep_ref, down_send_ref = outs
    up = dot_rows(pre_grad_ref[...], rows_ref[...])
    down = dot_rows(act_ref[...], grads_ref[...])
    rows = up.shape[0] // 4
    up_keep_ref[...] = up[: 2 * rows]
    up_send_ref[...] = up[2 * rows :].astype(LOW)
    down_keep_ref[:rows, :] = down[:rows]
    down_keep_ref[rows:, :] = down[2 * rows : 3 * rows]
    down_send_ref[:rows, :] = down[rows : 2 * rows].astype(LOW)
    down_send_ref[rows:, :] = down[3 * rows :].astype(LOW)


def after_kernel(parts, share, lines, *refs):
    place_ref, middle_ref, normed_ref, cot_ref, gain_ref, router_ref = refs[:6]
    out_refs = refs[6:10]
    came_refs = refs[10 : 10 + parts]
    branch_ref, block_ref, small_ref = refs[10 + parts : 13 + parts]
    grad_refs = refs[13 + parts :]
    if parts == 1:
        returned = came_refs[0][...].astype(WIDE)
    else:
        returned = join_shares(came_refs)
    expert_out, routed_grad = returned[:, :D], returned[:, D:]
    middle = middle_ref[...]
    scale = lax.rsqrt(jnp.mean(middle * middle, axis=-1, keepdims=True) + EPS_NORM)
    probs = route_probs(normed_ref[...], router_ref)
    count, experts = probs.shape
    row = lax.broadcasted_iota(jnp.int32, (count, experts), 0)
    col = lax.broadcasted_iota(jnp.int32, (count, experts), 1)
    chosen = jnp.zeros((count, experts), WIDE)
    for m in range(count // share):
        inside = (row >= m * share) & (row < (m + 1) * share)
        chosen = jnp.where(inside & (col == (place_ref[0] ^ m) // GROUP), 1.0, chosen)
    gate = jnp.sum(chosen * probs, axis=-1, keepdims=True)
    upstream = cot_ref[...].astype(WIDE)
    block_ref[...] = (middle + gate * expert_out).astype(LOW)
    gate_grad = jnp.sum(upstream * expert_out, axis=-1, keepdims=True)
    logit_grad = gate * (chosen - probs) * gate_grad
    router_term = jnp.dot(
        logit_grad, router_ref[...], precision=HIGH, preferred_element_type=WIDE
    )
    router_grad = lax.dot_general(
        logit_grad,
        normed_ref[...].astype(WIDE),
        (((0,), (0,)), ((), ())),
        precision=HIGH,
        preferred_element_type=WIDE,
    )
    normed_grad = routed_grad + router_term
    small_ref[...] = jnp.zeros_like(small_ref)
    small_ref[1 + HEADS : 2 + HEADS, :] = jnp.sum(
        normed_grad * middle * scale, axis=0, keepdims=True
    )
    small_ref[2 + HEADS : 2 + HEADS + experts, :] = router_grad
    weighted = normed_grad * gain_ref[...]
    inner = jnp.mean(weighted * middle, axis=-1, keepdims=True)
    middle_grad = upstream + scale * weighted - middle * scale * scale * scale * inner
    branch = middle_grad.astype(LOW)
    branch_ref[...] = branch
    for m in range(4):
        grad_refs[m][...] = dot_cols(branch, out_refs[m][...]).astype(LOW)


def backward_kernel(*refs):
    slot_ref, proj_ref, probs_ref, hits_ref = refs[:4]
    grad_refs = refs[4:8]
    pg_ref, table_ref, sums_ref = refs[8:11]
    width = grad_refs[0].shape[1]
    heads = width // HEAD_DIM
    slots = jnp.concatenate([ref[...] for ref in grad_refs], axis=0)
    grad = dot_rows(slot_hits(slot_ref[...], slots.shape[0]), slots).astype(LOW)
    query = proj_ref[:, :width]
    key = proj_ref[:, width : 2 * width]
    value = proj_ref[:, 2 * width : 3 * width]
    row = lax.broadcasted_iota(jnp.int32, (SEQ_LEN, SEQ_LEN), 0)
    col = lax.broadcasted_iota(jnp.int32, (SEQ_LEN, SEQ_LEN), 1)
    mirror = jnp.where(row + col == SEQ_LEN - 1, 1.0, 0.0).astype(LOW)
    zero = jnp.zeros((SEQ_LEN, width), WIDE)
    query_grad, key_grad, value_grad = zero, zero, zero
    sums_ref[...] = jnp.zeros_like(sums_ref)
    for h, mask in enumerate(head_masks(width)):
        probs = probs_ref[h]
        picked = grad * jnp.where(mask, 1.0, 0.0).astype(LOW)
        prob_grad = dot_cols(picked, value)
        inner = jnp.sum(probs * prob_grad, axis=-1, keepdims=True)
        score_grad = (probs * (prob_grad - inner)).astype(LOW)
        value_grad = jnp.where(mask, dot_rows(probs.astype(LOW), grad), value_grad)
        key_grad = jnp.where(mask, dot_rows(score_grad, query), key_grad)
        query_grad = jnp.where(mask, dot_plain(score_grad, key), query_grad)
        mirrored = dot_rows(score_grad, mirror)
        wide = jnp.concatenate([mirrored, jnp.zeros((SEQ_LEN, SEQ_LEN), WIDE)], axis=1)
        turned = pltpu.roll(wide, 0, 1, stride=1, stride_axis=0)
        sums_ref[h : h + 1, :] = jnp.sum(turned, axis=0, keepdims=True)
    pg_ref[:, :width] = (query_grad * HEAD_DIM ** (-0.5)).astype(LOW)
    pg_ref[:, width : 2 * width] = (key_grad * HEAD_DIM ** (-0.5)).astype(LOW)
    pg_ref[:, 2 * width : 3 * width] = value_grad.astype(LOW)
    table_ref[...] = jnp.dot(sums_ref[...], hits_ref[...], precision=HIGH)


def weights_kernel(parts, heads, *refs):
    place_ref, pg_ref, n_ref, w_ref, x_ref, gain_ref, table_ref, small_ref = refs[:8]
    mixed_refs = refs[8:12]
    branch_refs = refs[12:16]
    keep_ref, send_ref = refs[16:18]
    outs = refs[18:-2]
    wide_ref, total_ref = refs[-2:]
    width = mixed_refs[0].shape[1]
    place, tensor_place = place_ref[0], place_ref[1]
    wide_ref[...] = dot_cols(pg_ref[...], w_ref[:, : 3 * width])
    values = x_ref[...].astype(WIDE)
    scale = lax.rsqrt(jnp.mean(values * values, axis=-1, keepdims=True) + EPS_NORM)
    gain_grad = jnp.sum(wide_ref[...] * values * scale, axis=0, keepdims=True)
    quarter = SEQ_LEN // 4
    for half, distance in enumerate((0, 2)):
        near = pl.multiple_of((tensor_place ^ distance) * quarter, quarter)
        far = pl.multiple_of((tensor_place ^ distance ^ 1) * quarter, quarter)
        block = pl.ds(half * quarter, quarter)
        keep_ref[block, :] = wide_ref[pl.ds(near, quarter), :]
        send_ref[block, :] = wide_ref[pl.ds(far, quarter), :].astype(LOW)
    small = small_ref[...]
    line = lax.broadcasted_iota(jnp.int32, (small.shape[0], 1), 0)
    small = jnp.where(line == 0, gain_grad, small)
    for h in range(heads):
        counts = jnp.concatenate(
            [table_ref[h : h + 1, :], jnp.zeros((1, D - table_ref.shape[1]), WIDE)], axis=1
        )
        small = jnp.where(line == 1 + tensor_place * heads + h, counts, small)
    mixed = jnp.concatenate([ref[...] for ref in mixed_refs], axis=0)
    branch = jnp.concatenate([ref[...] for ref in branch_refs], axis=0)
    total_ref[:, : 3 * width] = dot_rows(n_ref[...], pg_ref[...])
    total_ref[:, 3 * width :] = dot_rows(branch, mixed)
    if parts == 1:
        outs[0][...] = total_ref[...].astype(LOW)
        outs[1][...] = small.astype(LOW)
    else:
        rows = D // parts
        for m in range(parts):
            at = pl.multiple_of((place ^ m) * rows, rows)
            outs[m][:rows, :] = total_ref[pl.ds(at, rows), :].astype(LOW)
            outs[m][rows:, :] = small.astype(LOW)


def gather_projections(own, place, count):
    if count != 8:
        return [lax.all_gather(own, "expert", axis=0, tiled=True)]
    pieces = [own] + [None] * (count - 1)
    pieces[1] = swap(own, "expert", 1)
    for m in range(2, count, 2):
        pieces[m] = swap(own, "expert", m)
    for m in range(2, count, 2):
        pieces[m + 1] = swap(pieces[m], "expert", 1)
    return pieces


def gather_group(up, down):
    up_near, down_far = swap(up, "expert", 1), swap(down, "expert", 2)
    up_far = swap(jnp.concatenate([up, up_near], 0), "expert", 2)
    down_near = swap(jnp.concatenate([down, down_far], 0), "expert", 1)
    return [up, up_near, up_far], [down, down_far, down_near]


def reduce_group(up_keep, up_send, down_keep, down_send):
    rows = up_keep.shape[0] // 2
    up_half = up_keep + swap(up_send, "expert", 2).astype(WIDE)
    down_half = down_keep + swap(down_send, "expert", 1).astype(WIDE)
    up_last = swap(up_half[rows:].astype(LOW), "expert", 1).astype(WIDE)
    down_last = swap(down_half[rows:].astype(LOW), "expert", 2).astype(WIDE)
    return up_half[:rows] + up_last, down_half[:rows] + down_last


def join(shares):
    count, (share, width) = len(shares), shares[0].shape
    if count > 8:
        return jnp.concatenate(shares, 0)
    return call(join_kernel, [shape_of(LOW, count * share, width)], shares)[0]


def body(
    block_input,
    cotangent,
    lengths,
    routes,
    norm_gains,
    gains_mean,
    gains_square,
    position_bias,
    bias_mean,
    bias_square,
    router,
    router_mean,
    router_square,
    qkv_weight,
    qkv_mean,
    qkv_square,
    out_weight,
    out_mean,
    out_square,
    expert_up,
    up_mean,
    up_square,
    expert_down,
    down_mean,
    down_square,
):
    tensor_size = lax.axis_size("tensor")
    tensor_place = lax.axis_index("tensor")
    expert_size = lax.axis_size("expert")
    place = lax.axis_index("expert")
    experts = expert_size // GROUP
    capacity = max(2, 9 * SEQ_LEN // (8 * expert_size))
    share = -(-capacity // tensor_size)
    own_slots = expert_size * share
    fan_down = max(1, FF // (experts * experts))
    heads_here = HEADS // tensor_size
    width = heads_here * HEAD_DIM
    rows_here = SEQ_LEN // tensor_size
    parts = expert_size if expert_size == 8 else 1
    shard = D // expert_size

    own_shard = jnp.concatenate(
        [qkv_weight[0], qkv_weight[1], qkv_weight[2], out_weight.T], axis=1
    ).astype(LOW)
    pieces = gather_projections(own_shard, place, expert_size)

    target = routes[:, 0]
    replica_hit = target[:, None] == jnp.arange(expert_size, dtype=jnp.int32)[None, :]
    ranks = jnp.cumsum(replica_hit.astype(jnp.int32), axis=0) - 1
    rank = jnp.sum(jnp.where(replica_hit, ranks, 0), axis=-1)
    slot = (
        ((rank // share) ^ tensor_place) * own_slots + (target ^ place) * share + rank % share
    )
    slot_row = slot[None, :]
    scalars = jnp.stack([place, tensor_place]).astype(jnp.int32)

    offsets = np.arange(2 * SEQ_LEN)
    circular = np.where(offsets < SEQ_LEN, offsets, offsets - 2 * SEQ_LEN)
    table = lax.dynamic_slice_in_dim(position_bias, tensor_place * heads_here, heads_here, 1)
    offset_bias = lax.dot_general(
        table, jnp.asarray(offset_hits(circular, BUCKETS)), (((0,), (1,)), ((), ())), precision=HIGH
    )
    normed_one, bias, own_inputs, own_upstream = call(
        prepare_kernel,
        [
            shape_of(LOW, SEQ_LEN, D),
            shape_of(WIDE, heads_here, SEQ_LEN, SEQ_LEN),
            shape_of(LOW, own_slots, D),
            shape_of(LOW, own_slots, D),
        ],
        [block_input, cotangent, norm_gains[0:1], slot_row, offset_bias],
    )
    own_shares = own_upstream.reshape(expert_size, share, D)
    grad_blocks = tensor_blocks(join(exchange([own_shares[m] for m in range(expert_size)])))

    outs = call(
        functools.partial(forward_kernel, parts),
        [
            shape_of(LOW, D, D),
            shape_of(LOW, SEQ_LEN, 3 * width),
            shape_of(WIDE, heads_here, SEQ_LEN, SEQ_LEN),
        ]
        + [shape_of(LOW, own_slots, width)] * 4,
        [place[None].astype(jnp.int32), lengths, normed_one, bias, slot_row] + pieces,
        scalars=2,
    )
    projections, projected, probs = outs[:3]
    mixed_blocks = outs[3:]
    out_blocks = tensor_blocks(projections[:, 3 * width :].T)
    ups, downs = gather_group(expert_up[0].astype(LOW), expert_down[0].astype(LOW))
    router_rows = router.T

    mixed_own = [mixed_blocks[0]] + [swap(mixed_blocks[m], "tensor", m) for m in range(1, 4)]
    cut = expert_size if expert_size <= 8 else 0
    middle, normed_two, *shares = call(
        middle_kernel,
        [shape_of(WIDE, own_slots, D), shape_of(LOW, own_slots, D)]
        + [shape_of(LOW, share, D)] * cut,
        [own_inputs, norm_gains[1:2]] + mixed_own + out_blocks,
    )
    if cut == 0:
        shares = normed_two.reshape(expert_size, share, D)
        shares = [shares[m] for m in range(expert_size)]
    row_blocks = tensor_blocks(join(exchange(shares)))

    hidden = 4 * expert_up.shape[1]
    rows_in, grad_rows, act, grad_pre, keep, send = call(
        expert_kernel,
        [
            shape_of(LOW, 4 * own_slots, D),
            shape_of(LOW, 4 * own_slots, D),
            shape_of(LOW, 4 * own_slots, hidden),
            shape_of(LOW, 4 * own_slots, hidden),
            shape_of(WIDE, 2 * own_slots, 2 * D),
            shape_of(LOW, 2 * own_slots, 2 * D),
        ],
        [scalars, router_rows] + row_blocks + grad_blocks + ups + downs,
        scalars=1,
    )
    half = keep + swap(send, "tensor", 1).astype(WIDE)
    whole = half[:own_slots] + swap(half[own_slots:].astype(LOW), "tensor", 2).astype(WIDE)
    shares = whole.astype(LOW).reshape(expert_size, share, 2 * D)
    came = exchange([shares[m] for m in range(expert_size)])
    if cut == 0:
        came = [jnp.concatenate(came, 0)]
    half_up = shape_of(WIDE, hidden // 2, D)
    sent_up = shape_of(LOW, hidden // 2, D)
    up_grad, down_grad = reduce_group(
        *call(
            expert_weights_kernel,
            [half_up, sent_up, half_up, sent_up],
            [rows_in, grad_rows, act, grad_pre],
        )
    )

    lines = -(-(2 + HEADS + experts) // 16) * 16
    branch_grad, block_slots, small, *mixed_grads = call(
        functools.partial(after_kernel, len(came), share, lines),
        [
            shape_of(LOW, own_slots, D),
            shape_of(LOW, own_slots, D),
            shape_of(WIDE, lines, D),
        ]
        + [shape_of(LOW, own_slots, width)] * 4,
        [scalars, middle, normed_two, own_upstream, norm_gains[1:2], router_rows]
        + out_blocks
        + came,
        scalars=1,
    )
    mixed_grads = [mixed_grads[0]] + [swap(mixed_grads[m], "tensor", m) for m in range(1, 4)]
    branch_blocks = tensor_blocks(branch_grad)
    block_blocks = tensor_blocks(block_slots)

    mirrored = np.arange(2 * SEQ_LEN) - (SEQ_LEN - 1)
    projected_grad, table_grad, _ = call(
        backward_kernel,
        [
            shape_of(LOW, SEQ_LEN, 3 * width),
            shape_of(WIDE, 8, 128),
            shape_of(WIDE, 8, 2 * SEQ_LEN),
        ],
        [slot_row, projected, probs, jnp.asarray(offset_hits(mirrored, 128))] + mixed_grads,
    )
    if parts == 1:
        grad_shapes = [shape_of(LOW, D, D), shape_of(LOW, lines, D)]
    else:
        grad_shapes = [shape_of(LOW, shard + lines, D)] * parts
    keep, send, *grad_pieces = call(
        functools.partial(weights_kernel, parts, heads_here),
        [shape_of(WIDE, 2 * rows_here, D), shape_of(LOW, 2 * rows_here, D)] + grad_shapes,
        [
            scalars,
            projected_grad,
            normed_one,
            projections,
            block_input,
            norm_gains[0:1],
            table_grad,
            small,
        ]
        + list(mixed_blocks)
        + branch_blocks,
        scalars=1,
        scratch=[pltpu.VMEM((SEQ_LEN, D), WIDE), pltpu.VMEM((D, D), WIDE)],
    )
    if parts == 1:
        order = place ^ jnp.arange(expert_size, dtype=jnp.int32)
        cut = jnp.take(grad_pieces[0].reshape(expert_size, shard, D), order, axis=0)
        grad_pieces = [jnp.concatenate([cut[m], grad_pieces[1]], 0) for m in range(expert_size)]
    grad_came = exchange(grad_pieces)

    half = keep + swap(send, "tensor", 1).astype(WIDE)
    normed_one_grad = half[:rows_here] + swap(half[rows_here:].astype(LOW), "tensor", 2).astype(
        WIDE
    )
    own_start = tensor_place * rows_here
    slot_own = lax.dynamic_slice_in_dim(slot, own_start, rows_here, 0)
    own_hits = (
        slot_own[:, None] == jnp.arange(tensor_size * own_slots, dtype=jnp.int32)[None, :]
    ).astype(LOW)
    block_output = dot_plain(own_hits, jnp.concatenate(block_blocks, 0)).astype(LOW)
    middle_own = dot_plain(own_hits, jnp.concatenate(branch_blocks, 0))
    inputs_own = lax.dynamic_slice_in_dim(block_input, own_start, rows_here, 0).astype(WIDE)
    scale_own = lax.rsqrt(jnp.mean(inputs_own * inputs_own, axis=-1, keepdims=True) + EPS_NORM)
    weighted = normed_one_grad * norm_gains[0]
    inner = jnp.mean(weighted * inputs_own, axis=-1, keepdims=True)
    input_grad = (
        middle_own
        + scale_own * weighted
        - inputs_own * scale_own * scale_own * scale_own * inner
    )

    total = grad_came[0].astype(WIDE)
    for m in range(1, expert_size):
        total = total + grad_came[m].astype(WIDE)
    qkv_grad = jnp.stack([total[:shard, c * width : (c + 1) * width] for c in range(3)])
    out_grad = total[:shard, 3 * width :].T
    small = total[shard:]
    small = small + swap(small, "tensor", 1)
    small = small + swap(small, "tensor", 2)
    gains_grad = jnp.concatenate([small[0:1], small[1 + HEADS : 2 + HEADS]], 0)
    bias_grad = small[1 : 1 + HEADS, :BUCKETS].T
    router_grad = small[2 + HEADS : 2 + HEADS + experts].T

    new_gains_mean, new_gains_square, new_norm_gains = adamw(
        norm_gains, gains_mean, gains_square, gains_grad, 0.3, 0.0
    )
    new_bias_mean, new_bias_square, new_position_bias = adamw(
        position_bias, bias_mean, bias_square, bias_grad, 1.5, 0.0
    )
    new_router_mean, new_router_square, new_router = adamw(
        router, router_mean, router_square, router_grad, 3.0 * (2 * D) ** (-0.5), DECAY
    )
    new_qkv_mean, new_qkv_square, new_qkv_weight = adamw(
        qkv_weight, qkv_mean, qkv_square, qkv_grad, 3.0 * D ** (-0.5), DECAY
    )
    new_out_mean, new_out_square, new_out_weight = adamw(
        out_weight, out_mean, out_square, out_grad, 3.0 * FAN_O ** (-0.5), DECAY
    )
    new_up_mean, new_up_square, new_expert_up = adamw(
        expert_up, up_mean, up_square, up_grad[None], 3.0 * D ** (-0.5), DECAY
    )
    new_down_mean, new_down_square, new_expert_down = adamw(
        expert_down, down_mean, down_square, down_grad[None], 3.0 * fan_down ** (-0.5), DECAY
    )
    return (
        block_output,
        input_grad,
        new_gains_mean,
        new_gains_square,
        new_norm_gains,
        new_bias_mean,
        new_bias_square,
        new_position_bias,
        new_router_mean,
        new_router_square,
        new_router,
        new_qkv_mean,
        new_qkv_square,
        new_qkv_weight,
        new_out_mean,
        new_out_square,
        new_out_weight,
        new_up_mean,
        new_up_square,
        new_expert_up,
        new_down_mean,
        new_down_square,
        new_expert_down,
    )


def solution(mesh):
    return jax.shard_map(
        body,
        mesh=mesh,
        in_specs=(
            P("expert", None),
            P("expert", None),
            P("expert"),
            P("expert", None),
            P(),
            P(),
            P(),
            P(),
            P(),
            P(),
            P(),
            P(),
            P(),
            P(None, "expert", "tensor"),
            P(None, "expert", "tensor"),
            P(None, "expert", "tensor"),
            P("tensor", "expert"),
            P("tensor", "expert"),
            P("tensor", "expert"),
            P("expert", "tensor", None),
            P("expert", "tensor", None),
            P("expert", "tensor", None),
            P("expert", "tensor", None),
            P("expert", "tensor", None),
            P("expert", "tensor", None),
        ),
        out_specs=(
            P(("expert", "tensor"), None),
            P(("expert", "tensor"), None),
            P(),
            P(),
            P(),
            P(),
            P(),
            P(),
            P(),
            P(),
            P(),
            P(None, "expert", "tensor"),
            P(None, "expert", "tensor"),
            P(None, "expert", "tensor"),
            P("tensor", "expert"),
            P("tensor", "expert"),
            P("tensor", "expert"),
            P("expert", "tensor", None),
            P("expert", "tensor", None),
            P("expert", "tensor", None),
            P("expert", "tensor", None),
            P("expert", "tensor", None),
            P("expert", "tensor", None),
        ),
        check_vma=False,
    )
```

```python
import functools

import jax
import jax.numpy as jnp
import numpy as np
from jax import lax
from jax.experimental import pallas as pl
from jax.experimental.pallas import tpu as pltpu
from jax.sharding import PartitionSpec as P

D = 768
HEADS = 12
HEAD_DIM = 64
FF = 3072
BUCKETS = 32
MAX_DIST = 128
GROUP = 4
STEP = 10
SEQ_LEN = 512
FAN_O = 3


EPS_NORM = 1e-06
BETA_ONE = 0.9
BETA_TWO = 0.999
EPS_ADAM = 1e-08
DECAY = 0.01
MASKED = -1e30
HIGH = lax.Precision.HIGHEST
LIMIT_SMALL = 40 * 2**20
LIMIT_LARGE = 56 * 2**20
LOW = jnp.bfloat16
WIDE = jnp.float32


FOLD_ORDERS = ((0, 2, 4, 6), (1, 3, 5, 7), (0, 1, 4, 5), (2, 3, 6, 7))


def tie(*groups):
    return lax.optimization_barrier(groups)


def swap(block, axis, distance):
    count = lax.axis_size(axis)
    return lax.ppermute(block, axis, [(low, low ^ distance) for low in range(count)])


def exchange(rows):
    return lax.all_to_all(rows, "expert", split_axis=0, concat_axis=0, tiled=True)


def tensor_blocks(block):
    far = swap(block, "tensor", 2)
    near = swap(block, "tensor", 1)
    return [block, near, far, swap(far, "tensor", 1)]


def bucket_of(offset):
    half = BUCKETS // 2
    exact = half // 2
    distance = np.abs(offset)
    far = np.full(offset.shape, exact, np.int32)
    for level in range(exact + 1, half):
        limit = int(
            np.ceil(exact * (MAX_DIST / exact) ** ((level - exact) / (half - exact)) - 1e-09)
        )
        far = far + (distance >= limit)
    return np.where(offset > 0, half, 0) + np.where(distance < exact, distance, far)


def offset_hits(offsets, width):
    hits = (bucket_of(offsets)[:, None] == np.arange(width)[None, :]) & (
        np.abs(offsets)[:, None] < SEQ_LEN
    )
    return hits.astype(np.float32)


def adamw(weight, mean, square, grad, rate, decay):
    mean_new = BETA_ONE * mean + (1.0 - BETA_ONE) * grad
    square_new = BETA_TWO * square + (1.0 - BETA_TWO) * grad * grad
    mean_hat = mean_new / (1.0 - BETA_ONE**STEP)
    square_hat = square_new / (1.0 - BETA_TWO**STEP)
    weight_new = weight - rate * (mean_hat / (jnp.sqrt(square_hat) + EPS_ADAM) + decay * weight)
    return (mean_new, square_new, weight_new)


def dot_rows(left, right):
    return lax.dot_general(left, right, (((0,), (0,)), ((), ())), preferred_element_type=WIDE)


def dot_cols(left, right):
    return lax.dot_general(left, right, (((1,), (1,)), ((), ())), preferred_element_type=WIDE)


def dot_plain(left, right):
    return jnp.dot(left, right, preferred_element_type=WIDE)


def call(
    kernel, outs, operands, micros, scalars=0, scratch=(), away=(), away_outs=(), limit=LIMIT_LARGE
):
    vmem = pl.BlockSpec(memory_space=pltpu.VMEM)
    hbm = pl.BlockSpec(memory_space=pltpu.HBM)
    smem = pl.BlockSpec(memory_space=pltpu.SMEM)
    return pl.pallas_call(
        kernel,
        out_shape=outs,
        in_specs=[
            smem if at < scalars else hbm if at in away else vmem for at in range(len(operands))
        ],
        out_specs=[hbm if at in away_outs else vmem for at in range(len(outs))],
        scratch_shapes=list(scratch),
        compiler_params=pltpu.CompilerParams(vmem_limit_bytes=limit),
        cost_estimate=pl.CostEstimate(
            flops=int(micros * 9e8), bytes_accessed=0, transcendentals=0
        ),
    )(*operands)


def start_copies(sources, targets, sems, first=0):
    copies = [
        pltpu.make_async_copy(source, target, sems.at[first + at])
        for at, (source, target) in enumerate(zip(sources, targets))
    ]
    for copy in copies:
        copy.start()
    return copies


def wait_copies(copies):
    for copy in copies:
        copy.wait()


def shape_of(dtype, *sizes):
    return jax.ShapeDtypeStruct(sizes, dtype)


def head_masks(width):
    lane = lax.broadcasted_iota(jnp.int32, (1, width), 1)
    return [
        (lane >= h * HEAD_DIM) & (lane < (h + 1) * HEAD_DIM) for h in range(width // HEAD_DIM)
    ]


def slot_hits(slot_row, count):
    slots = lax.broadcasted_iota(jnp.int32, (count, slot_row.shape[1]), 0)
    return jnp.where(slots == slot_row, 1.0, 0.0).astype(LOW)


def shard_kernel(qkv_far, out_far, shard_ref, qkv_ref, out_ref, sems):
    wait_copies(start_copies([qkv_far, out_far], [qkv_ref, out_ref], sems))
    width = qkv_ref.shape[2]
    for c in range(3):
        shard_ref[:, c * width : (c + 1) * width] = qkv_ref[c].astype(LOW)
    row = lax.broadcasted_iota(jnp.int32, (width, width), 0)
    col = lax.broadcasted_iota(jnp.int32, (width, width), 1)
    same = jnp.where(row == col, 1.0, 0.0).astype(LOW)
    shard_ref[:, 3 * width :] = dot_rows(out_ref[...].astype(LOW), same).astype(LOW)


def prepare_kernel(
    share,
    place_ref,
    target_ref,
    gain_ref,
    spread_ref,
    bias_ref,
    circular_ref,
    x_far,
    cot_far,
    up_far,
    down_far,
    n_ref,
    offset_ref,
    slot_ref,
    xs_ref,
    cs_far,
    cot_out_ref,
    up_out,
    down_out,
    x_ref,
    cot_ref,
    up_ref,
    down_ref,
    cs_ref,
    up_low_ref,
    down_low_ref,
    sems,
):
    first = start_copies([x_far, cot_far], [x_ref, cot_ref], sems)
    second = start_copies([up_far, down_far], [up_ref, down_ref], sems, 2)
    own_slots = xs_ref.shape[0]
    target = target_ref[...]
    replica = lax.broadcasted_iota(jnp.int32, (own_slots // share, SEQ_LEN), 0)
    named = jnp.where(replica == target, 1.0, 0.0)
    row = lax.broadcasted_iota(jnp.int32, (SEQ_LEN, SEQ_LEN), 0)
    col = lax.broadcasted_iota(jnp.int32, (SEQ_LEN, SEQ_LEN), 1)
    upto = jnp.where(row < col, 1.0, 0.0).astype(LOW)
    ranks = dot_plain(named.astype(LOW), upto)
    rank = jnp.sum(named * ranks, axis=0, keepdims=True).astype(jnp.int32)
    owner = jnp.zeros_like(rank)
    for m in range(1, 4):
        owner = owner + jnp.where(rank >= m * share, 1, 0)
    slot = (owner ^ place_ref[1]) * own_slots + target * share + rank - owner * share
    slot_ref[...] = slot
    hits = slot_hits(slot, own_slots)
    wait_copies(first)
    xs_ref[...] = dot_plain(hits, x_ref[...]).astype(LOW)
    own = dot_plain(hits, cot_ref[...]).astype(LOW)
    cs_ref[...] = own
    cot_out_ref[...] = dot_rows(spread_ref[...], own).astype(LOW)
    third = start_copies([cs_ref], [cs_far], sems, 4)
    values = x_ref[...].astype(WIDE)
    scale = lax.rsqrt(jnp.mean(values * values, axis=-1, keepdims=True) + EPS_NORM)
    n_ref[...] = (values * scale * gain_ref[...]).astype(LOW)
    heads = lax.dot_general(
        bias_ref[...],
        circular_ref[...],
        (((0,), (0,)), ((), ())),
        precision=HIGH,
        preferred_element_type=WIDE,
    )
    for h in range(offset_ref.shape[0]):
        row = lax.broadcasted_iota(jnp.int32, (heads.shape[0], 1), 0)
        here = row == place_ref[1] * offset_ref.shape[0] + h
        offset_ref[h : h + 1, :] = jnp.sum(jnp.where(here, heads, 0.0), axis=0, keepdims=True)
    wait_copies(second)
    up_low_ref[...] = up_ref[0].astype(LOW)
    down_low_ref[...] = down_ref[0].astype(LOW)
    wait_copies(third + start_copies([up_low_ref, down_low_ref], [up_out, down_out], sems, 5))


def assemble_kernel(parts, place_ref, *refs):
    pieces = refs[:parts]
    w_ref, out_ref, sems = refs[parts:]
    rows = D // parts
    copies = []
    for m in range(parts):
        at = pl.multiple_of((place_ref[0] ^ m) * rows, rows) if parts > 1 else 0
        copy = pltpu.make_async_copy(pieces[m], w_ref.at[pl.ds(at, rows), :], sems.at[m])
        copy.start()
        copies.append(copy)
    for copy in copies:
        copy.wait()
    width = out_ref.shape[0]
    row = lax.broadcasted_iota(jnp.int32, (width, width), 0)
    col = lax.broadcasted_iota(jnp.int32, (width, width), 1)
    same = jnp.where(row == col, 1.0, 0.0).astype(LOW)
    out_ref[...] = dot_cols(same, w_ref[:, 3 * width :]).astype(LOW)


def forward_kernel(length_ref, n_ref, offset_ref, slot_ref, w_ref, *refs):
    proj_far, probs_far = refs[:2]
    mixed_refs = refs[2:6]
    proj_ref, probs_ref, sems = refs[6:]
    width = mixed_refs[0].shape[1]
    proj_ref[...] = dot_plain(n_ref[...], w_ref[:, : 3 * width]).astype(LOW)
    copies = start_copies([proj_ref], [proj_far], sems)
    query = proj_ref[:, :width]
    key = proj_ref[:, width : 2 * width]
    value = proj_ref[:, 2 * width : 3 * width]
    live = lax.broadcasted_iota(jnp.int32, (1, SEQ_LEN), 1) < length_ref[0]
    mixed = jnp.zeros((SEQ_LEN, width), WIDE)
    for h, mask in enumerate(head_masks(width)):
        picked = query * jnp.where(mask, 1.0, 0.0).astype(LOW)
        line = jnp.broadcast_to(offset_ref[h : h + 1, :], (SEQ_LEN, 2 * SEQ_LEN))
        bias = pltpu.roll(line, 0, 1, stride=1, stride_axis=0)[:, :SEQ_LEN]
        scores = dot_cols(picked, key) * HEAD_DIM ** (-0.5) + bias
        scores = jnp.where(live, scores, MASKED)
        expo = jnp.exp(scores - jnp.max(scores, axis=-1, keepdims=True))
        probs = expo * (1.0 / jnp.sum(expo, axis=-1, keepdims=True))
        probs_ref[h] = probs.astype(LOW)
        copies += start_copies([probs_ref.at[h]], [probs_far.at[h]], sems, 1 + h)
        mixed = jnp.where(mask, dot_plain(probs_ref[h], value), mixed)
    count = mixed_refs[0].shape[0]
    hits = slot_hits(slot_ref[...], 4 * count)
    slots = dot_plain(hits, mixed.astype(LOW)).astype(LOW)
    for m in range(4):
        mixed_refs[m][...] = slots[m * count : (m + 1) * count, :]
    wait_copies(copies)


def join_kernel(spread_ref, came_ref, rows_ref):
    rows_ref[...] = dot_plain(spread_ref[...], came_ref[...]).astype(LOW)


def route_probs(rows, router_ref):
    logits = lax.dot_general(
        rows.astype(WIDE),
        router_ref[...],
        (((1,), (1,)), ((), ())),
        precision=HIGH,
        preferred_element_type=WIDE,
    )
    expo = jnp.exp(logits - jnp.max(logits, axis=-1, keepdims=True))
    return expo / jnp.sum(expo, axis=-1, keepdims=True)


def middle_kernel(x_ref, gain_ref, spread_ref, *refs):
    mixed_refs, out_refs = refs[:4], refs[4:8]
    middle_ref, normed_ref, sent_ref = refs[8:]
    middle = x_ref[...].astype(WIDE)
    for m in range(4):
        middle = middle + dot_plain(mixed_refs[m][...], out_refs[m][...])
    middle_ref[...] = middle
    scale = lax.rsqrt(jnp.mean(middle * middle, axis=-1, keepdims=True) + EPS_NORM)
    normed = (middle * scale * gain_ref[...]).astype(LOW)
    normed_ref[...] = normed
    sent_ref[...] = dot_rows(spread_ref[...], normed).astype(LOW)


def expert_kernel(*refs):
    place_ref, router_ref = refs[:2]
    row_refs, cot_refs = refs[2:6], refs[6:10]
    up_refs, down_refs = refs[10:13], refs[13:16]
    rows_ref, grads_ref, act_ref, pre_grad_ref = refs[16:20]
    keep_ref, send_ref = refs[20:22]
    weight_up = jnp.concatenate([ref[...] for ref in up_refs], axis=0)
    near, far, pair = down_refs
    shard = near.shape[0]
    weight_down = jnp.concatenate([near[...], pair[:shard, :], far[...], pair[shard:, :]], axis=0)
    count = row_refs[0].shape[0]
    for at, m in enumerate((0, 2, 1, 3)):
        rows_ref[at * count : (at + 1) * count, :] = row_refs[m][...]
        grads_ref[at * count : (at + 1) * count, :] = cot_refs[m][...]
    rows = rows_ref[...]
    probs = route_probs(rows, router_ref)
    here = lax.broadcasted_iota(jnp.int32, (1, probs.shape[1]), 1) == place_ref[0] // GROUP
    gate = jnp.sum(jnp.where(here, probs, 0.0), axis=-1, keepdims=True)
    grads_ref[...] = (gate * grads_ref[...].astype(WIDE)).astype(LOW)
    pre = dot_cols(rows, weight_up)
    root = np.sqrt(2 / np.pi).astype(np.float32)
    bend = np.float32(0.044715)
    square = pre * pre
    curve = jnp.tanh(root * (pre + bend * square * pre))
    act_ref[...] = (0.5 * pre * (1.0 + curve)).astype(LOW)
    slope = 0.5 * (1.0 + curve) + 0.5 * pre * (1.0 - curve * curve) * root * (
        1.0 + 3.0 * bend * square
    )
    pre_grad_ref[...] = (slope * dot_cols(grads_ref[...], weight_down)).astype(LOW)
    out = dot_plain(act_ref[...], weight_down)
    back = dot_plain(pre_grad_ref[...], weight_up)
    keep_ref[:, :D] = out[: 2 * count]
    keep_ref[:, D:] = back[: 2 * count]
    send_ref[:, :D] = out[2 * count :].astype(LOW)
    send_ref[:, D:] = back[2 * count :].astype(LOW)


def reduce_kernel(*refs):
    for at in range(2):
        keep_ref, came_ref = refs[2 * at : 2 * at + 2]
        half_ref, sent_ref = refs[4 + 2 * at : 6 + 2 * at]
        rows = half_ref.shape[0]
        half_ref[...] = keep_ref[:rows, :] + came_ref[:rows, :].astype(WIDE)
        sent_ref[...] = (keep_ref[rows:, :] + came_ref[rows:, :].astype(WIDE)).astype(LOW)


def expert_update_kernel(rates, up_half_ref, up_last_ref, down_half_ref, down_last_ref, *refs):
    sources, results, held, made, sems = refs[:6], refs[6:12], refs[12:18], refs[18:24], refs[24]
    first = start_copies(sources[:3], held[:3], sems)
    second = start_copies(sources[3:], held[3:], sems, 3)
    copies = []
    for at, (half_ref, last_ref, fetched) in enumerate(
        ((up_half_ref, up_last_ref, first), (down_half_ref, down_last_ref, second))
    ):
        wait_copies(fetched)
        grad = half_ref[...] + last_ref[...].astype(WIDE)
        here = slice(3 * at, 3 * at + 3)
        values = adamw(*[ref[0] for ref in held[here]], grad, rates[at], DECAY)
        for ref, value in zip(made[here], values):
            ref[0] = value
        copies += start_copies(made[here], results[here], sems, 6 + 3 * at)
    wait_copies(copies)


def input_half_kernel(keep_ref, came_ref, kept_ref, sent_ref):
    rows = SEQ_LEN // 4
    kept_ref[:rows, :] = keep_ref[:rows, :] + came_ref[:rows, :].astype(WIDE)
    kept_ref[rows:, :] = keep_ref[2 * rows :, :] + came_ref[2 * rows :, :].astype(WIDE)
    far = keep_ref[rows : 2 * rows, :] + came_ref[rows : 2 * rows, :].astype(WIDE)
    sent_ref[:rows, :] = far.astype(LOW)
    sent_ref[rows:, :] = kept_ref[rows:, :].astype(LOW)


def half_kernel(keep_ref, came_ref, kept_ref, sent_ref):
    rows = kept_ref.shape[0]
    kept_ref[...] = keep_ref[:rows, :] + came_ref[:rows, :].astype(WIDE)
    sent_ref[...] = (keep_ref[rows:, :] + came_ref[rows:, :].astype(WIDE)).astype(LOW)


def spread_kernel(kept_ref, came_ref, spread_ref, sent_ref):
    whole = (kept_ref[...] + came_ref[...].astype(WIDE)).astype(LOW)
    sent_ref[...] = dot_rows(spread_ref[...], whole).astype(LOW)


def expert_weights_kernel(rows_ref, grads_ref, act_ref, pre_grad_ref, *outs):
    up_keep_ref, up_send_ref, down_keep_ref, down_send_ref = outs
    up = dot_rows(pre_grad_ref[...], rows_ref[...])
    down = dot_rows(act_ref[...], grads_ref[...])
    rows = up.shape[0] // 4
    up_keep_ref[...] = up[: 2 * rows]
    up_send_ref[...] = up[2 * rows :].astype(LOW)
    down_keep_ref[:rows, :] = down[:rows]
    down_keep_ref[rows:, :] = down[2 * rows : 3 * rows]
    down_send_ref[:rows, :] = down[rows : 2 * rows].astype(LOW)
    down_send_ref[rows:, :] = down[3 * rows :].astype(LOW)


def after_kernel(share, *refs):
    middle_ref, normed_ref, cot_ref, gain_ref, router_ref, spread_ref, came_ref = refs[:7]
    out_refs = refs[7:11]
    branch_ref, block_ref, small_ref = refs[11:14]
    grad_refs = refs[14:]
    returned = dot_plain(spread_ref[...], came_ref[...])
    expert_out, routed_grad = returned[:, :D], returned[:, D:]
    middle = middle_ref[...]
    scale = lax.rsqrt(jnp.mean(middle * middle, axis=-1, keepdims=True) + EPS_NORM)
    probs = route_probs(normed_ref[...], router_ref)
    count, experts = probs.shape
    row = lax.broadcasted_iota(jnp.int32, (count, experts), 0)
    col = lax.broadcasted_iota(jnp.int32, (count, experts), 1)
    chosen = jnp.zeros((count, experts), WIDE)
    for m in range(count // share):
        inside = (row >= m * share) & (row < (m + 1) * share)
        chosen = jnp.where(inside & (col == m // GROUP), 1.0, chosen)
    gate = jnp.sum(chosen * probs, axis=-1, keepdims=True)
    upstream = cot_ref[...].astype(WIDE)
    block_ref[...] = (middle + gate * expert_out).astype(LOW)
    gate_grad = jnp.sum(upstream * expert_out, axis=-1, keepdims=True)
    logit_grad = gate * (chosen - probs) * gate_grad
    router_term = jnp.dot(
        logit_grad, router_ref[...], precision=HIGH, preferred_element_type=WIDE
    )
    router_grad = lax.dot_general(
        logit_grad,
        normed_ref[...].astype(WIDE),
        (((0,), (0,)), ((), ())),
        precision=HIGH,
        preferred_element_type=WIDE,
    )
    normed_grad = routed_grad + router_term
    small_ref[...] = jnp.zeros_like(small_ref)
    small_ref[1 + HEADS : 2 + HEADS, :] = jnp.sum(
        normed_grad * middle * scale, axis=0, keepdims=True
    )
    small_ref[2 + HEADS : 2 + HEADS + experts, :] = router_grad
    weighted = normed_grad * gain_ref[...]
    inner = jnp.mean(weighted * middle, axis=-1, keepdims=True)
    middle_grad = upstream + scale * weighted - middle * scale * scale * scale * inner
    branch = middle_grad.astype(LOW)
    branch_ref[...] = branch
    for m in range(4):
        grad_refs[m][...] = dot_cols(branch, out_refs[m][...]).astype(LOW)


def backward_kernel(*refs):
    slot_ref, proj_ref, probs_ref, hits_ref = refs[:4]
    grad_refs = refs[4:8]
    pg_ref, table_ref, sums_ref = refs[8:11]
    width = grad_refs[0].shape[1]
    heads = width // HEAD_DIM
    slots = jnp.concatenate([ref[...] for ref in grad_refs], axis=0)
    grad = dot_rows(slot_hits(slot_ref[...], slots.shape[0]), slots).astype(LOW)
    query = proj_ref[:, :width]
    key = proj_ref[:, width : 2 * width]
    value = proj_ref[:, 2 * width : 3 * width]
    row = lax.broadcasted_iota(jnp.int32, (SEQ_LEN, SEQ_LEN), 0)
    col = lax.broadcasted_iota(jnp.int32, (SEQ_LEN, SEQ_LEN), 1)
    mirror = jnp.where(row + col == SEQ_LEN - 1, 1.0, 0.0).astype(LOW)
    zero = jnp.zeros((SEQ_LEN, width), WIDE)
    query_grad, key_grad, value_grad = zero, zero, zero
    sums_ref[...] = jnp.zeros_like(sums_ref)
    for h, mask in enumerate(head_masks(width)):
        probs_low = probs_ref[h]
        probs = probs_low.astype(WIDE)
        picked = grad * jnp.where(mask, 1.0, 0.0).astype(LOW)
        prob_grad = dot_cols(picked, value)
        inner = jnp.sum(probs * prob_grad, axis=-1, keepdims=True)
        score_grad = (probs * (prob_grad - inner)).astype(LOW)
        value_grad = jnp.where(mask, dot_rows(probs_low, grad), value_grad)
        key_grad = jnp.where(mask, dot_rows(score_grad, query), key_grad)
        query_grad = jnp.where(mask, dot_plain(score_grad, key), query_grad)
        mirrored = dot_rows(score_grad, mirror)
        wide = jnp.concatenate([mirrored, jnp.zeros((SEQ_LEN, SEQ_LEN), WIDE)], axis=1)
        turned = pltpu.roll(wide, 0, 1, stride=1, stride_axis=0)
        sums_ref[h : h + 1, :] = jnp.sum(turned, axis=0, keepdims=True)
    pg_ref[:, :width] = (query_grad * HEAD_DIM ** (-0.5)).astype(LOW)
    pg_ref[:, width : 2 * width] = (key_grad * HEAD_DIM ** (-0.5)).astype(LOW)
    pg_ref[:, 2 * width : 3 * width] = value_grad.astype(LOW)
    table_ref[...] = jnp.dot(sums_ref[...], hits_ref[...], precision=HIGH)


def weights_kernel(parts, place_ref, n_ref, pg_ref, *refs):
    mixed_refs, branch_refs, outs, total_ref = refs[:4], refs[4:8], refs[8:-1], refs[-1]
    width = mixed_refs[0].shape[1]
    total_ref[:, : 3 * width] = dot_rows(n_ref[...], pg_ref[...]).astype(LOW)
    mixed = jnp.concatenate([ref[...] for ref in mixed_refs], axis=0)
    branch = jnp.concatenate([ref[...] for ref in branch_refs], axis=0)
    total_ref[:, 3 * width :] = dot_rows(branch, mixed).astype(LOW)
    if parts == 1:
        outs[0][...] = total_ref[...]
    else:
        rows = D // parts
        for ref, half, order in zip(outs, (0, 0, 1, 1), FOLD_ORDERS):
            for at, m in enumerate(order):
                source = pl.multiple_of((place_ref[0] ^ m) * rows, rows)
                ref[at * rows : (at + 1) * rows, :] = total_ref[
                    pl.ds(source, rows), half * D // 2 : (half + 1) * D // 2
                ]


def fold_kernel(*refs):
    for at in range(2):
        keep_ref, came_ref = refs[2 * at : 2 * at + 2]
        kept_ref, sent_ref = refs[4 + 2 * at : 6 + 2 * at]
        rows = kept_ref.shape[0] // 2
        for block in range(4):
            here = slice(block * rows, (block + 1) * rows)
            to = slice(block // 2 * rows, (block // 2 + 1) * rows)
            total = keep_ref[here, :].astype(WIDE) + came_ref[here, :].astype(WIDE)
            if block % 2 == 0:
                kept_ref[to, :] = total
            else:
                sent_ref[to, :] = total.astype(LOW)


def last_fold_kernel(*refs):
    kept_ref, sent_ref = refs[4:]
    for at in range(2):
        keep_ref, came_ref = refs[2 * at : 2 * at + 2]
        rows, width = kept_ref.shape[0], keep_ref.shape[1]
        cols = slice(at * width, (at + 1) * width)
        total = keep_ref[...] + came_ref[...].astype(WIDE)
        kept_ref[:, cols] = total[:rows]
        sent_ref[:, cols] = total[rows:].astype(LOW)


def input_kernel(
    heads,
    place_ref,
    pg_ref,
    w_ref,
    x_ref,
    gain_ref,
    table_ref,
    early_ref,
    keep_ref,
    send_ref,
    wide_ref,
):
    tensor_place = place_ref[1]
    width = heads * HEAD_DIM
    wide_ref[...] = dot_cols(pg_ref[...], w_ref[:, : 3 * width])
    values = x_ref[...].astype(WIDE)
    scale = lax.rsqrt(jnp.mean(values * values, axis=-1, keepdims=True) + EPS_NORM)
    gain_grad = jnp.sum(wide_ref[...] * values * scale, axis=0, keepdims=True)
    quarter = SEQ_LEN // 4
    for half, distance in enumerate((0, 2)):
        near = pl.multiple_of((tensor_place ^ distance) * quarter, quarter)
        far = pl.multiple_of((tensor_place ^ distance ^ 1) * quarter, quarter)
        block = pl.ds(half * quarter, quarter)
        keep_ref[block, :] = wide_ref[pl.ds(near, quarter), :]
        send_ref[block, :] = wide_ref[pl.ds(far, quarter), :].astype(LOW)
    small = early_ref[...]
    line = lax.broadcasted_iota(jnp.int32, (small.shape[0], 1), 0)
    small = jnp.where(line == 0, gain_grad, small)
    for h in range(heads):
        counts = jnp.concatenate(
            [table_ref[h : h + 1, :], jnp.zeros((1, D - table_ref.shape[1]), WIDE)], axis=1
        )
        small = jnp.where(line == 1 + tensor_place * heads + h, counts, small)
    keep_ref[SEQ_LEN // 2 :, :] = small
    send_ref[SEQ_LEN // 2 :, :] = small.astype(LOW)


def update_kernel(*refs):
    came, weights, outs = refs[:-12], refs[-12:-6], refs[-6:]
    shard = weights[0].shape[1]
    total = jnp.zeros((shard, D), WIDE)
    for ref in came:
        for m in range(ref.shape[0] // shard):
            total = total + ref[m * shard : (m + 1) * shard, :].astype(WIDE)
    width = weights[0].shape[2]
    for c in range(3):
        grad = total[:, c * width : (c + 1) * width]
        made = adamw(*[ref[c] for ref in weights[:3]], grad, 3.0 * D ** (-0.5), DECAY)
        for ref, value in zip(outs[:3], made):
            ref[c] = value
    grad = jnp.transpose(total[:, 3 * width :])
    made = adamw(*[ref[...] for ref in weights[3:]], grad, 3.0 * FAN_O ** (-0.5), DECAY)
    for ref, value in zip(outs[3:], made):
        ref[...] = value


def gather_projections(own, ready, count):
    if count != 8:
        return [lax.all_gather(own, "expert", axis=0, tiled=True)], ready
    pieces = [own] + [None] * (count - 1)
    for m in range(count - 2, 0, -2):
        pieces[m] = swap(own, "expert", m)
    pieces[1] = swap(own, "expert", 1)
    pieces[2], ready = tie(pieces[2], ready)
    for m in range(2, count, 2):
        pieces[m + 1] = swap(pieces[m], "expert", 1)
    return pieces, ready


def body(
    block_input,
    cotangent,
    lengths,
    routes,
    norm_gains,
    gains_mean,
    gains_square,
    position_bias,
    bias_mean,
    bias_square,
    router,
    router_mean,
    router_square,
    qkv_weight,
    qkv_mean,
    qkv_square,
    out_weight,
    out_mean,
    out_square,
    expert_up,
    up_mean,
    up_square,
    expert_down,
    down_mean,
    down_square,
):
    tensor_size = lax.axis_size("tensor")
    tensor_place = lax.axis_index("tensor")
    expert_size = lax.axis_size("expert")
    place = lax.axis_index("expert")
    experts = expert_size // GROUP
    capacity = max(2, 9 * SEQ_LEN // (8 * expert_size))
    share = -(-capacity // tensor_size)
    own_slots = expert_size * share
    fan_down = max(1, FF // (experts * experts))
    heads_here = HEADS // tensor_size
    width = heads_here * HEAD_DIM
    rows_here = SEQ_LEN // tensor_size
    parts = expert_size if expert_size == 8 else 1
    shard = D // expert_size
    padded = -(-share // 8) * 8
    lines = -(-(2 + HEADS + experts) // 16) * 16
    scalars = jnp.stack([place, tensor_place]).astype(jnp.int32)

    own_shard = call(
        shard_kernel,
        [shape_of(LOW, shard, D)],
        [qkv_weight, out_weight],
        1,
        away=(0, 1),
        scratch=[
            pltpu.VMEM(qkv_weight.shape, WIDE),
            pltpu.VMEM(out_weight.shape, WIDE),
            pltpu.SemaphoreType.DMA((2,)),
        ],
    )[0]

    spread = np.zeros((expert_size, share, expert_size, padded), np.float32)
    for e in range(expert_size):
        spread[e, np.arange(share), e, np.arange(share)] = 1.0
    spread = jnp.asarray(spread.reshape(own_slots, expert_size * padded), LOW)
    offsets = np.arange(2 * SEQ_LEN)
    circular = np.where(offsets < SEQ_LEN, offsets, offsets - 2 * SEQ_LEN)
    circular_hits = jnp.asarray(offset_hits(circular, BUCKETS).T)
    half = expert_up.shape[1:]
    prepared = call(
        functools.partial(prepare_kernel, share),
        [
            shape_of(LOW, SEQ_LEN, D),
            shape_of(WIDE, heads_here, 2 * SEQ_LEN),
            shape_of(jnp.int32, 1, SEQ_LEN),
            shape_of(LOW, own_slots, D),
            shape_of(LOW, own_slots, D),
            shape_of(LOW, expert_size * padded, D),
            shape_of(LOW, *half),
            shape_of(LOW, *half),
        ],
        [
            scalars,
            routes.reshape(1, SEQ_LEN),
            norm_gains[0:1],
            spread,
            position_bias,
            circular_hits,
            block_input,
            cotangent,
            expert_up,
            expert_down,
        ],
        4,
        scalars=1,
        away=(6, 7, 8, 9),
        away_outs=(4, 6, 7),
        scratch=[
            pltpu.VMEM((SEQ_LEN, D), LOW),
            pltpu.VMEM((SEQ_LEN, D), LOW),
            pltpu.VMEM(expert_up.shape, WIDE),
            pltpu.VMEM(expert_up.shape, WIDE),
            pltpu.VMEM((own_slots, D), LOW),
            pltpu.VMEM(half, LOW),
            pltpu.VMEM(half, LOW),
            pltpu.SemaphoreType.DMA((7,)),
        ],
    )
    with jax.named_scope("cot_dispatch"):
        cot_came = exchange(prepared[5])
    prepared = prepared[:5] + prepared[6:]
    with jax.named_scope("projection_gather"):
        pieces, prepared = gather_projections(own_shard, prepared, expert_size)
    normed_one, offset_bias, slot_row, own_inputs, own_upstream, up_low, down_low = prepared
    joined = [shape_of(LOW, own_slots, D)]
    if parts > 1:
        down_low, pieces[6] = tie(down_low, pieces[6])
    with jax.named_scope("expert_gather"):
        down_far = swap(down_low, "expert", 2)
    projections, out_here = call(
        functools.partial(assemble_kernel, parts),
        [shape_of(LOW, D, D), shape_of(LOW, width, D)],
        [scalars] + pieces,
        1,
        scalars=1,
        scratch=[pltpu.SemaphoreType.DMA((parts,))],
        away=range(1, 1 + parts),
    )
    up_low, out_here = tie(up_low, out_here)
    with jax.named_scope("expert_gather"):
        up_near = swap(up_low, "expert", 1)
    with jax.named_scope("out_blocks"):
        out_blocks = tensor_blocks(out_here)
    projected, probs, *mixed_blocks = call(
        forward_kernel,
        [
            shape_of(LOW, SEQ_LEN, 3 * width),
            shape_of(LOW, heads_here, SEQ_LEN, SEQ_LEN),
        ]
        + [shape_of(LOW, own_slots, width)] * 4,
        [lengths, normed_one, offset_bias, slot_row, projections],
        6,
        scalars=1,
        away_outs=(0, 1),
        scratch=[
            pltpu.VMEM((SEQ_LEN, 3 * width), LOW),
            pltpu.VMEM((heads_here, SEQ_LEN, SEQ_LEN), LOW),
            pltpu.SemaphoreType.DMA((1 + heads_here,)),
        ],
    )
    router_rows = router.T

    mixed_blocks, up_near, down_far, cot_came = tie(mixed_blocks, up_near, down_far, cot_came)
    with jax.named_scope("expert_gather"):
        up_far = swap(jnp.concatenate([up_low, up_near], 0), "expert", 2)
        down_near = swap(jnp.concatenate([down_low, down_far], 0), "expert", 1)
    ups, downs = [up_low, up_near, up_far], [down_low, down_far, down_near]
    with jax.named_scope("mixed"):
        mixed_own = [mixed_blocks[0]] + [swap(mixed_blocks[m], "tensor", m) for m in range(1, 4)]
    own_cot = call(join_kernel, joined, [spread, cot_came], 1, limit=LIMIT_SMALL)[0]
    with jax.named_scope("cot_blocks"):
        grad_blocks = tensor_blocks(own_cot)

    middle, normed_two, rows_sent = call(
        middle_kernel,
        [
            shape_of(WIDE, own_slots, D),
            shape_of(LOW, own_slots, D),
            shape_of(LOW, expert_size * padded, D),
        ],
        [own_inputs, norm_gains[1:2], spread] + mixed_own + out_blocks,
        1,
    )
    with jax.named_scope("row_dispatch"):
        rows_came = exchange(rows_sent)
    own_rows = call(join_kernel, joined, [spread, rows_came], 1, limit=LIMIT_SMALL)[0]
    with jax.named_scope("row_blocks"):
        row_blocks = tensor_blocks(own_rows)

    hidden = 4 * expert_up.shape[1]
    rows_in, grad_rows, act, grad_pre, keep, send = call(
        expert_kernel,
        [
            shape_of(LOW, 4 * own_slots, D),
            shape_of(LOW, 4 * own_slots, D),
            shape_of(LOW, 4 * own_slots, hidden),
            shape_of(LOW, 4 * own_slots, hidden),
            shape_of(WIDE, 2 * own_slots, 2 * D),
            shape_of(LOW, 2 * own_slots, 2 * D),
        ],
        [scalars, router_rows] + row_blocks + grad_blocks + ups + downs,
        8,
        scalars=1,
        limit=LIMIT_SMALL,
    )
    half_up = shape_of(WIDE, hidden // 2, D)
    sent_up = shape_of(LOW, hidden // 2, D)
    up_keep, up_send, down_keep, down_send = call(
        expert_weights_kernel,
        [half_up, sent_up, half_up, sent_up],
        [rows_in, grad_rows, act, grad_pre],
        3,
        limit=LIMIT_SMALL,
    )
    with jax.named_scope("return_sum"):
        came = swap(send, "tensor", 1)
    came, up_send, down_send = tie(came, up_send, down_send)
    with jax.named_scope("expert_reduce"):
        up_came = swap(up_send, "expert", 2)
        down_came = swap(down_send, "expert", 1)
    kept, send = call(
        half_kernel,
        [shape_of(WIDE, own_slots, 2 * D), shape_of(LOW, own_slots, 2 * D)],
        [keep, came],
        1,
        limit=LIMIT_SMALL,
    )
    with jax.named_scope("return_sum"):
        came = swap(send, "tensor", 2)
    sent = call(
        spread_kernel,
        [shape_of(LOW, expert_size * padded, 2 * D)],
        [kept, came, spread],
        1,
        limit=LIMIT_SMALL,
    )[0]
    sent, up_came, down_came = tie(sent, up_came, down_came)
    with jax.named_scope("row_return"):
        returned = exchange(sent)
    quarter = (hidden // 4, D)
    up_half, up_send, down_half, down_send = call(
        reduce_kernel,
        [shape_of(WIDE, *quarter), shape_of(LOW, *quarter)] * 2,
        [up_keep, up_came, down_keep, down_came],
        1,
        limit=LIMIT_SMALL,
    )
    with jax.named_scope("expert_reduce"):
        up_last = swap(up_send, "expert", 1)
        down_last = swap(down_send, "expert", 2)

    branch_grad, block_slots, early, *mixed_grads = call(
        functools.partial(after_kernel, share),
        [
            shape_of(LOW, own_slots, D),
            shape_of(LOW, own_slots, D),
            shape_of(WIDE, lines, D),
        ]
        + [shape_of(LOW, own_slots, width)] * 4,
        [middle, normed_two, own_upstream, norm_gains[1:2], router_rows, spread, returned]
        + out_blocks,
        4,
    )
    with jax.named_scope("mixed_grad"):
        mixed_grads = [mixed_grads[0]] + [swap(mixed_grads[m], "tensor", m) for m in range(1, 4)]
    state = pltpu.VMEM(expert_up.shape, WIDE)
    (
        new_up_mean,
        new_up_square,
        new_expert_up,
        new_down_mean,
        new_down_square,
        new_expert_down,
    ) = call(
        functools.partial(
            expert_update_kernel, (3.0 * D ** (-0.5), 3.0 * fan_down ** (-0.5))
        ),
        [shape_of(WIDE, *expert_up.shape)] * 6,
        [
            up_half,
            up_last,
            down_half,
            down_last,
            expert_up,
            up_mean,
            up_square,
            expert_down,
            down_mean,
            down_square,
        ],
        4,
        away=range(4, 10),
        away_outs=range(6),
        scratch=[state] * 12 + [pltpu.SemaphoreType.DMA((12,))],
    )
    mixed_grads, branch_grad, new_up_mean, new_down_mean = tie(
        mixed_grads, branch_grad, new_up_mean, new_down_mean
    )
    with jax.named_scope("branch_blocks"):
        branch_far = swap(branch_grad, "tensor", 2)
        branch_near = swap(branch_grad, "tensor", 1)
    mirrored = np.arange(2 * SEQ_LEN) - (SEQ_LEN - 1)
    projected_grad, table_grad, _ = call(
        backward_kernel,
        [
            shape_of(LOW, SEQ_LEN, 3 * width),
            shape_of(WIDE, 8, 128),
            shape_of(WIDE, 8, 2 * SEQ_LEN),
        ],
        [slot_row, projected, probs, jnp.asarray(offset_hits(mirrored, 128))] + mixed_grads,
        5,
    )
    branch_far, projected_grad, block_slots = tie(branch_far, projected_grad, block_slots)
    with jax.named_scope("branch_blocks"):
        branch_both = swap(branch_far, "tensor", 1)
    with jax.named_scope("block_blocks"):
        block_blocks = tensor_blocks(block_slots)

    branch_blocks = [branch_grad, branch_near, branch_far, branch_both]
    grad_sent = call(
        functools.partial(weights_kernel, parts),
        [shape_of(LOW, D, D)] if parts == 1 else [shape_of(LOW, D // 2, D // 2)] * 4,
        [scalars, normed_one, projected_grad] + list(mixed_blocks) + branch_blocks,
        2,
        scalars=1,
        scratch=[pltpu.VMEM((D, D), LOW)],
    )
    grad_sent, projected_grad = tie(grad_sent, projected_grad)
    with jax.named_scope("projection_reduce"):
        if parts == 1:
            grad_came = [exchange(grad_sent[0])]
        else:
            one_keep, one_sent, two_keep, two_sent = grad_sent
            one_came, two_came = swap(one_sent, "expert", 1), swap(two_sent, "expert", 2)
            one_keep, one_sent, two_keep, two_sent = call(
                fold_kernel,
                [shape_of(WIDE, D // 4, D // 2), shape_of(LOW, D // 4, D // 2)] * 2,
                [one_keep, one_came, two_keep, two_came],
                1,
                limit=LIMIT_SMALL,
            )
            one_came, two_came = swap(one_sent, "expert", 2), swap(two_sent, "expert", 1)
            grad_kept, sent = call(
                last_fold_kernel,
                [shape_of(WIDE, shard, D), shape_of(LOW, shard, D)],
                [one_keep, one_came, two_keep, two_came],
                1,
                limit=LIMIT_SMALL,
            )
            grad_came = [grad_kept, swap(sent, "expert", 4)]
    keep, send = call(
        functools.partial(input_kernel, heads_here),
        [
            shape_of(WIDE, 2 * rows_here + lines, D),
            shape_of(LOW, 2 * rows_here + lines, D),
        ],
        [
            scalars,
            projected_grad,
            projections,
            block_input,
            norm_gains[0:1],
            table_grad,
            early,
        ],
        2,
        scalars=1,
        scratch=[pltpu.VMEM((SEQ_LEN, D), WIDE)],
    )
    with jax.named_scope("input_sum"):
        came = swap(send, "tensor", 1)
    kept, send = call(
        input_half_kernel,
        [shape_of(WIDE, rows_here + lines, D), shape_of(LOW, rows_here + lines, D)],
        [keep, came],
        1,
    )
    with jax.named_scope("input_sum"):
        came = swap(send, "tensor", 2)
        small = kept[rows_here:] + came[rows_here:].astype(WIDE)
        grad_came, came = tie(grad_came, came)
        normed_one_grad = kept[:rows_here] + came[:rows_here].astype(WIDE)
    with jax.named_scope("small_sum"):
        small = exchange(jnp.tile(small.astype(LOW), (expert_size, 1))).astype(WIDE)
        small = jnp.sum(small.reshape(expert_size, lines, D), axis=0)
    own_start = tensor_place * rows_here
    slot_own = lax.dynamic_slice_in_dim(slot_row[0], own_start, rows_here, 0)
    own_hits = (
        slot_own[:, None] == jnp.arange(tensor_size * own_slots, dtype=jnp.int32)[None, :]
    ).astype(LOW)
    block_output = dot_plain(own_hits, jnp.concatenate(block_blocks, 0)).astype(LOW)
    middle_own = dot_plain(own_hits, jnp.concatenate(branch_blocks, 0))
    inputs_own = lax.dynamic_slice_in_dim(block_input, own_start, rows_here, 0).astype(WIDE)
    scale_own = lax.rsqrt(jnp.mean(inputs_own * inputs_own, axis=-1, keepdims=True) + EPS_NORM)
    weighted = normed_one_grad * norm_gains[0]
    inner = jnp.mean(weighted * inputs_own, axis=-1, keepdims=True)
    input_grad = (
        middle_own
        + scale_own * weighted
        - inputs_own * scale_own * scale_own * scale_own * inner
    )

    gains_grad = jnp.concatenate([small[0:1], small[1 + HEADS : 2 + HEADS]], 0)
    bias_grad = small[1 : 1 + HEADS, :BUCKETS].T
    router_grad = small[2 + HEADS : 2 + HEADS + experts].T

    new_gains_mean, new_gains_square, new_norm_gains = adamw(
        norm_gains, gains_mean, gains_square, gains_grad, 0.3, 0.0
    )
    new_bias_mean, new_bias_square, new_position_bias = adamw(
        position_bias, bias_mean, bias_square, bias_grad, 1.5, 0.0
    )
    new_router_mean, new_router_square, new_router = adamw(
        router, router_mean, router_square, router_grad, 3.0 * (2 * D) ** (-0.5), DECAY
    )
    new_qkv_mean, new_qkv_square, new_qkv_weight, new_out_mean, new_out_square, new_out_weight = (
        call(
            update_kernel,
            [shape_of(WIDE, *qkv_weight.shape)] * 3 + [shape_of(WIDE, *out_weight.shape)] * 3,
            grad_came
            + [
                qkv_weight,
                qkv_mean,
                qkv_square,
                out_weight,
                out_mean,
                out_square,
            ],
            40,
            )
    )
    return (
        block_output,
        input_grad,
        new_gains_mean,
        new_gains_square,
        new_norm_gains,
        new_bias_mean,
        new_bias_square,
        new_position_bias,
        new_router_mean,
        new_router_square,
        new_router,
        new_qkv_mean,
        new_qkv_square,
        new_qkv_weight,
        new_out_mean,
        new_out_square,
        new_out_weight,
        new_up_mean,
        new_up_square,
        new_expert_up,
        new_down_mean,
        new_down_square,
        new_expert_down,
    )


def solution(mesh):
    return jax.shard_map(
        body,
        mesh=mesh,
        in_specs=(
            P("expert", None),
            P("expert", None),
            P("expert"),
            P("expert", None),
            P(),
            P(),
            P(),
            P(),
            P(),
            P(),
            P(),
            P(),
            P(),
            P(None, "expert", "tensor"),
            P(None, "expert", "tensor"),
            P(None, "expert", "tensor"),
            P("tensor", "expert"),
            P("tensor", "expert"),
            P("tensor", "expert"),
            P("expert", "tensor", None),
            P("expert", "tensor", None),
            P("expert", "tensor", None),
            P("expert", "tensor", None),
            P("expert", "tensor", None),
            P("expert", "tensor", None),
        ),
        out_specs=(
            P(("expert", "tensor"), None),
            P(("expert", "tensor"), None),
            P(),
            P(),
            P(),
            P(),
            P(),
            P(),
            P(),
            P(),
            P(),
            P(None, "expert", "tensor"),
            P(None, "expert", "tensor"),
            P(None, "expert", "tensor"),
            P("tensor", "expert"),
            P("tensor", "expert"),
            P("tensor", "expert"),
            P("expert", "tensor", None),
            P("expert", "tensor", None),
            P("expert", "tensor", None),
            P("expert", "tensor", None),
            P("expert", "tensor", None),
            P("expert", "tensor", None),
        ),
        check_vma=False,
    )
```

```python
import functools

import jax
import jax.numpy as jnp
import numpy as np
from jax import lax
from jax.experimental import pallas as pl
from jax.experimental.pallas import tpu as pltpu
from jax.sharding import PartitionSpec as P

D = 768
HEADS = 12
HEAD_DIM = 64
FF = 3072
BUCKETS = 32
MAX_DIST = 128
GROUP = 4
STEP = 10
SEQ_LEN = 512
FAN_O = 3


EPS_NORM = 1e-06
BETA_ONE = 0.9
BETA_TWO = 0.999
EPS_ADAM = 1e-08
DECAY = 0.01
MASKED = -1e30
HIGH = lax.Precision.HIGHEST
LIMIT_SMALL = 40 * 2**20
LIMIT_LARGE = 56 * 2**20
LOW = jnp.bfloat16
WIDE = jnp.float32


FOLD_ORDERS = ((0, 2, 4, 6), (1, 3, 5, 7), (0, 1, 4, 5), (2, 3, 6, 7))


def tie(*groups):
    return lax.optimization_barrier(groups)


def swap(block, axis, distance):
    count = lax.axis_size(axis)
    return lax.ppermute(block, axis, [(low, low ^ distance) for low in range(count)])


def exchange(rows):
    return lax.all_to_all(rows, "expert", split_axis=0, concat_axis=0, tiled=True)


def tensor_blocks(block):
    far = swap(block, "tensor", 2)
    near = swap(block, "tensor", 1)
    return [block, near, far, swap(far, "tensor", 1)]


def bucket_of(offset):
    half = BUCKETS // 2
    exact = half // 2
    distance = np.abs(offset)
    far = np.full(offset.shape, exact, np.int32)
    for level in range(exact + 1, half):
        limit = int(
            np.ceil(exact * (MAX_DIST / exact) ** ((level - exact) / (half - exact)) - 1e-09)
        )
        far = far + (distance >= limit)
    return np.where(offset > 0, half, 0) + np.where(distance < exact, distance, far)


def offset_hits(offsets, width):
    hits = (bucket_of(offsets)[:, None] == np.arange(width)[None, :]) & (
        np.abs(offsets)[:, None] < SEQ_LEN
    )
    return hits.astype(np.float32)


def adamw(weight, mean, square, grad, rate, decay):
    mean_new = BETA_ONE * mean + (1.0 - BETA_ONE) * grad
    square_new = BETA_TWO * square + (1.0 - BETA_TWO) * grad * grad
    mean_hat = mean_new / (1.0 - BETA_ONE**STEP)
    square_hat = square_new / (1.0 - BETA_TWO**STEP)
    weight_new = weight - rate * (mean_hat / (jnp.sqrt(square_hat) + EPS_ADAM) + decay * weight)
    return (mean_new, square_new, weight_new)


def dot_rows(left, right):
    return lax.dot_general(left, right, (((0,), (0,)), ((), ())), preferred_element_type=WIDE)


def dot_cols(left, right):
    return lax.dot_general(left, right, (((1,), (1,)), ((), ())), preferred_element_type=WIDE)


def dot_plain(left, right):
    return jnp.dot(left, right, preferred_element_type=WIDE)


def call(
    kernel, outs, operands, micros, scalars=0, scratch=(), away=(), away_outs=(), limit=LIMIT_LARGE
):
    vmem = pl.BlockSpec(memory_space=pltpu.VMEM)
    hbm = pl.BlockSpec(memory_space=pltpu.HBM)
    smem = pl.BlockSpec(memory_space=pltpu.SMEM)
    return pl.pallas_call(
        kernel,
        out_shape=outs,
        in_specs=[
            smem if at < scalars else hbm if at in away else vmem for at in range(len(operands))
        ],
        out_specs=[hbm if at in away_outs else vmem for at in range(len(outs))],
        scratch_shapes=list(scratch),
        compiler_params=pltpu.CompilerParams(vmem_limit_bytes=limit),
        cost_estimate=pl.CostEstimate(
            flops=int(micros * 9e8), bytes_accessed=0, transcendentals=0
        ),
    )(*operands)


def start_copies(sources, targets, sems, first=0):
    copies = [
        pltpu.make_async_copy(source, target, sems.at[first + at])
        for at, (source, target) in enumerate(zip(sources, targets))
    ]
    for copy in copies:
        copy.start()
    return copies


def wait_copies(copies):
    for copy in copies:
        copy.wait()


def shape_of(dtype, *sizes):
    return jax.ShapeDtypeStruct(sizes, dtype)


def head_masks(width):
    lane = lax.broadcasted_iota(jnp.int32, (1, width), 1)
    return [
        (lane >= h * HEAD_DIM) & (lane < (h + 1) * HEAD_DIM) for h in range(width // HEAD_DIM)
    ]


def slot_hits(slot_row, count):
    slots = lax.broadcasted_iota(jnp.int32, (count, slot_row.shape[1]), 0)
    return jnp.where(slots == slot_row, 1.0, 0.0).astype(LOW)


def shard_kernel(qkv_far, out_far, shard_ref, qkv_ref, out_ref, sems):
    wait_copies(start_copies([qkv_far, out_far], [qkv_ref, out_ref], sems))
    width = qkv_ref.shape[2]
    for c in range(3):
        shard_ref[:, c * width : (c + 1) * width] = qkv_ref[c].astype(LOW)
    row = lax.broadcasted_iota(jnp.int32, (width, width), 0)
    col = lax.broadcasted_iota(jnp.int32, (width, width), 1)
    same = jnp.where(row == col, 1.0, 0.0).astype(LOW)
    shard_ref[:, 3 * width :] = dot_rows(out_ref[...].astype(LOW), same).astype(LOW)


def prepare_kernel(
    share,
    place_ref,
    target_ref,
    gain_ref,
    spread_ref,
    bias_ref,
    circular_ref,
    x_far,
    cot_far,
    up_far,
    down_far,
    n_ref,
    offset_ref,
    slot_ref,
    xs_ref,
    cs_far,
    cot_out_ref,
    up_out,
    down_out,
    x_ref,
    cot_ref,
    up_ref,
    down_ref,
    cs_ref,
    up_low_ref,
    down_low_ref,
    sems,
):
    first = start_copies([x_far, cot_far], [x_ref, cot_ref], sems)
    second = start_copies([up_far, down_far], [up_ref, down_ref], sems, 2)
    own_slots = xs_ref.shape[0]
    target = target_ref[...]
    replica = lax.broadcasted_iota(jnp.int32, (own_slots // share, SEQ_LEN), 0)
    named = jnp.where(replica == target, 1.0, 0.0)
    row = lax.broadcasted_iota(jnp.int32, (SEQ_LEN, SEQ_LEN), 0)
    col = lax.broadcasted_iota(jnp.int32, (SEQ_LEN, SEQ_LEN), 1)
    upto = jnp.where(row < col, 1.0, 0.0).astype(LOW)
    ranks = dot_plain(named.astype(LOW), upto)
    rank = jnp.sum(named * ranks, axis=0, keepdims=True).astype(jnp.int32)
    owner = jnp.zeros_like(rank)
    for m in range(1, 4):
        owner = owner + jnp.where(rank >= m * share, 1, 0)
    slot = (owner ^ place_ref[1]) * own_slots + target * share + rank - owner * share
    slot_ref[...] = slot
    hits = slot_hits(slot, own_slots)
    wait_copies(first)
    xs_ref[...] = dot_plain(hits, x_ref[...]).astype(LOW)
    own = dot_plain(hits, cot_ref[...]).astype(LOW)
    cs_ref[...] = own
    cot_out_ref[...] = dot_rows(spread_ref[...], own).astype(LOW)
    third = start_copies([cs_ref], [cs_far], sems, 4)
    values = x_ref[...].astype(WIDE)
    scale = lax.rsqrt(jnp.mean(values * values, axis=-1, keepdims=True) + EPS_NORM)
    n_ref[...] = (values * scale * gain_ref[...]).astype(LOW)
    heads = lax.dot_general(
        bias_ref[...],
        circular_ref[...],
        (((0,), (0,)), ((), ())),
        precision=HIGH,
        preferred_element_type=WIDE,
    )
    for h in range(offset_ref.shape[0]):
        row = lax.broadcasted_iota(jnp.int32, (heads.shape[0], 1), 0)
        here = row == place_ref[1] * offset_ref.shape[0] + h
        offset_ref[h : h + 1, :] = jnp.sum(jnp.where(here, heads, 0.0), axis=0, keepdims=True)
    wait_copies(second)
    up_low_ref[...] = up_ref[0].astype(LOW)
    down_low_ref[...] = down_ref[0].astype(LOW)
    wait_copies(third + start_copies([up_low_ref, down_low_ref], [up_out, down_out], sems, 5))


def assemble_kernel(parts, place_ref, *refs):
    pieces = refs[:parts]
    w_ref, out_ref, sems = refs[parts:]
    rows = D // parts
    copies = []
    for m in range(parts):
        at = pl.multiple_of((place_ref[0] ^ m) * rows, rows) if parts > 1 else 0
        copy = pltpu.make_async_copy(pieces[m], w_ref.at[pl.ds(at, rows), :], sems.at[m])
        copy.start()
        copies.append(copy)
    for copy in copies:
        copy.wait()
    width = out_ref.shape[0]
    row = lax.broadcasted_iota(jnp.int32, (width, width), 0)
    col = lax.broadcasted_iota(jnp.int32, (width, width), 1)
    same = jnp.where(row == col, 1.0, 0.0).astype(LOW)
    out_ref[...] = dot_cols(same, w_ref[:, 3 * width :]).astype(LOW)


def forward_kernel(length_ref, n_ref, offset_ref, slot_ref, w_ref, *refs):
    proj_far, probs_far = refs[:2]
    mixed_refs = refs[2:6]
    proj_ref, probs_ref, sems = refs[6:]
    width = mixed_refs[0].shape[1]
    proj_ref[...] = dot_plain(n_ref[...], w_ref[:, : 3 * width]).astype(LOW)
    copies = start_copies([proj_ref], [proj_far], sems)
    query = proj_ref[:, :width]
    key = proj_ref[:, width : 2 * width]
    value = proj_ref[:, 2 * width : 3 * width]
    live = lax.broadcasted_iota(jnp.int32, (1, SEQ_LEN), 1) < length_ref[0]
    mixed = jnp.zeros((SEQ_LEN, width), WIDE)
    for h, mask in enumerate(head_masks(width)):
        picked = query * jnp.where(mask, 1.0, 0.0).astype(LOW)
        line = jnp.broadcast_to(offset_ref[h : h + 1, :], (SEQ_LEN, 2 * SEQ_LEN))
        bias = pltpu.roll(line, 0, 1, stride=1, stride_axis=0)[:, :SEQ_LEN]
        scores = dot_cols(picked, key) * HEAD_DIM ** (-0.5) + bias
        scores = jnp.where(live, scores, MASKED)
        expo = jnp.exp(scores - jnp.max(scores, axis=-1, keepdims=True))
        probs = expo * (1.0 / jnp.sum(expo, axis=-1, keepdims=True))
        probs_ref[h] = probs.astype(LOW)
        copies += start_copies([probs_ref.at[h]], [probs_far.at[h]], sems, 1 + h)
        mixed = jnp.where(mask, dot_plain(probs_ref[h], value), mixed)
    count = mixed_refs[0].shape[0]
    hits = slot_hits(slot_ref[...], 4 * count)
    slots = dot_plain(hits, mixed.astype(LOW)).astype(LOW)
    for m in range(4):
        mixed_refs[m][...] = slots[m * count : (m + 1) * count, :]
    wait_copies(copies)


def join_kernel(spread_ref, came_ref, rows_ref):
    rows_ref[...] = dot_plain(spread_ref[...], came_ref[...]).astype(LOW)


def route_probs(rows, router_ref):
    logits = lax.dot_general(
        rows.astype(WIDE),
        router_ref[...],
        (((1,), (1,)), ((), ())),
        precision=HIGH,
        preferred_element_type=WIDE,
    )
    expo = jnp.exp(logits - jnp.max(logits, axis=-1, keepdims=True))
    return expo / jnp.sum(expo, axis=-1, keepdims=True)


def middle_kernel(x_ref, gain_ref, spread_ref, *refs):
    mixed_refs, out_refs = refs[:4], refs[4:8]
    middle_ref, normed_ref, sent_ref = refs[8:]
    middle = x_ref[...].astype(WIDE)
    for m in range(4):
        middle = middle + dot_plain(mixed_refs[m][...], out_refs[m][...])
    middle_ref[...] = middle
    scale = lax.rsqrt(jnp.mean(middle * middle, axis=-1, keepdims=True) + EPS_NORM)
    normed = (middle * scale * gain_ref[...]).astype(LOW)
    normed_ref[...] = normed
    sent_ref[...] = dot_rows(spread_ref[...], normed).astype(LOW)


def expert_kernel(*refs):
    place_ref, router_ref = refs[:2]
    row_refs, cot_refs = refs[2:6], refs[6:10]
    up_refs, down_refs = refs[10:13], refs[13:16]
    rows_ref, grads_ref, act_ref, pre_grad_ref = refs[16:20]
    keep_ref, send_ref = refs[20:22]
    weight_up = jnp.concatenate([ref[...] for ref in up_refs], axis=0)
    near, far, pair = down_refs
    shard = near.shape[0]
    weight_down = jnp.concatenate([near[...], pair[:shard, :], far[...], pair[shard:, :]], axis=0)
    count = row_refs[0].shape[0]
    for at, m in enumerate((0, 2, 1, 3)):
        rows_ref[at * count : (at + 1) * count, :] = row_refs[m][...]
        grads_ref[at * count : (at + 1) * count, :] = cot_refs[m][...]
    rows = rows_ref[...]
    probs = route_probs(rows, router_ref)
    here = lax.broadcasted_iota(jnp.int32, (1, probs.shape[1]), 1) == place_ref[0] // GROUP
    gate = jnp.sum(jnp.where(here, probs, 0.0), axis=-1, keepdims=True)
    grads_ref[...] = (gate * grads_ref[...].astype(WIDE)).astype(LOW)
    pre = dot_cols(rows, weight_up)
    root = np.sqrt(2 / np.pi).astype(np.float32)
    bend = np.float32(0.044715)
    square = pre * pre
    curve = jnp.tanh(root * (pre + bend * square * pre))
    act_ref[...] = (0.5 * pre * (1.0 + curve)).astype(LOW)
    slope = 0.5 * (1.0 + curve) + 0.5 * pre * (1.0 - curve * curve) * root * (
        1.0 + 3.0 * bend * square
    )
    pre_grad_ref[...] = (slope * dot_cols(grads_ref[...], weight_down)).astype(LOW)
    out = dot_plain(act_ref[...], weight_down)
    back = dot_plain(pre_grad_ref[...], weight_up)
    keep_ref[:, :D] = out[: 2 * count]
    keep_ref[:, D:] = back[: 2 * count]
    send_ref[:, :D] = out[2 * count :].astype(LOW)
    send_ref[:, D:] = back[2 * count :].astype(LOW)


def reduce_kernel(*refs):
    for at in range(2):
        keep_ref, came_ref = refs[2 * at : 2 * at + 2]
        half_ref, sent_ref = refs[4 + 2 * at : 6 + 2 * at]
        rows = half_ref.shape[0]
        half_ref[...] = keep_ref[:rows, :] + came_ref[:rows, :].astype(WIDE)
        sent_ref[...] = (keep_ref[rows:, :] + came_ref[rows:, :].astype(WIDE)).astype(LOW)


def expert_update_kernel(rates, up_half_ref, up_last_ref, down_half_ref, down_last_ref, *refs):
    sources, results, held, made, sems = refs[:6], refs[6:12], refs[12:18], refs[18:24], refs[24]
    first = start_copies(sources[:3], held[:3], sems)
    second = start_copies(sources[3:], held[3:], sems, 3)
    copies = []
    for at, (half_ref, last_ref, fetched) in enumerate(
        ((up_half_ref, up_last_ref, first), (down_half_ref, down_last_ref, second))
    ):
        wait_copies(fetched)
        grad = half_ref[...] + last_ref[...].astype(WIDE)
        here = slice(3 * at, 3 * at + 3)
        values = adamw(*[ref[0] for ref in held[here]], grad, rates[at], DECAY)
        for ref, value in zip(made[here], values):
            ref[0] = value
        copies += start_copies(made[here], results[here], sems, 6 + 3 * at)
    wait_copies(copies)


def input_half_kernel(keep_ref, came_ref, kept_ref, sent_ref):
    rows = SEQ_LEN // 4
    kept_ref[:rows, :] = keep_ref[:rows, :] + came_ref[:rows, :].astype(WIDE)
    kept_ref[rows:, :] = keep_ref[2 * rows :, :] + came_ref[2 * rows :, :].astype(WIDE)
    far = keep_ref[rows : 2 * rows, :] + came_ref[rows : 2 * rows, :].astype(WIDE)
    sent_ref[:rows, :] = far.astype(LOW)
    sent_ref[rows:, :] = kept_ref[rows:, :].astype(LOW)


def half_kernel(keep_ref, came_ref, kept_ref, sent_ref):
    rows = kept_ref.shape[0]
    kept_ref[...] = keep_ref[:rows, :] + came_ref[:rows, :].astype(WIDE)
    sent_ref[...] = (keep_ref[rows:, :] + came_ref[rows:, :].astype(WIDE)).astype(LOW)


def spread_kernel(kept_ref, came_ref, spread_ref, sent_ref):
    whole = (kept_ref[...] + came_ref[...].astype(WIDE)).astype(LOW)
    sent_ref[...] = dot_rows(spread_ref[...], whole).astype(LOW)


def expert_weights_kernel(rows_ref, grads_ref, act_ref, pre_grad_ref, *outs):
    up_keep_ref, up_send_ref, down_keep_ref, down_send_ref = outs
    up = dot_rows(pre_grad_ref[...], rows_ref[...])
    down = dot_rows(act_ref[...], grads_ref[...])
    rows = up.shape[0] // 4
    up_keep_ref[...] = up[: 2 * rows]
    up_send_ref[...] = up[2 * rows :].astype(LOW)
    down_keep_ref[:rows, :] = down[:rows]
    down_keep_ref[rows:, :] = down[2 * rows : 3 * rows]
    down_send_ref[:rows, :] = down[rows : 2 * rows].astype(LOW)
    down_send_ref[rows:, :] = down[3 * rows :].astype(LOW)


def after_kernel(share, *refs):
    middle_ref, normed_ref, cot_ref, gain_ref, router_ref, spread_ref, came_ref = refs[:7]
    out_refs = refs[7:11]
    branch_ref, block_ref, small_ref = refs[11:14]
    grad_refs = refs[14:]
    returned = dot_plain(spread_ref[...], came_ref[...])
    expert_out, routed_grad = returned[:, :D], returned[:, D:]
    middle = middle_ref[...]
    scale = lax.rsqrt(jnp.mean(middle * middle, axis=-1, keepdims=True) + EPS_NORM)
    probs = route_probs(normed_ref[...], router_ref)
    count, experts = probs.shape
    row = lax.broadcasted_iota(jnp.int32, (count, experts), 0)
    col = lax.broadcasted_iota(jnp.int32, (count, experts), 1)
    chosen = jnp.zeros((count, experts), WIDE)
    for m in range(count // share):
        inside = (row >= m * share) & (row < (m + 1) * share)
        chosen = jnp.where(inside & (col == m // GROUP), 1.0, chosen)
    gate = jnp.sum(chosen * probs, axis=-1, keepdims=True)
    upstream = cot_ref[...].astype(WIDE)
    block_ref[...] = (middle + gate * expert_out).astype(LOW)
    gate_grad = jnp.sum(upstream * expert_out, axis=-1, keepdims=True)
    logit_grad = gate * (chosen - probs) * gate_grad
    router_term = jnp.dot(
        logit_grad, router_ref[...], precision=HIGH, preferred_element_type=WIDE
    )
    router_grad = lax.dot_general(
        logit_grad,
        normed_ref[...].astype(WIDE),
        (((0,), (0,)), ((), ())),
        precision=HIGH,
        preferred_element_type=WIDE,
    )
    normed_grad = routed_grad + router_term
    small_ref[...] = jnp.zeros_like(small_ref)
    small_ref[1 + HEADS : 2 + HEADS, :] = jnp.sum(
        normed_grad * middle * scale, axis=0, keepdims=True
    )
    small_ref[2 + HEADS : 2 + HEADS + experts, :] = router_grad
    weighted = normed_grad * gain_ref[...]
    inner = jnp.mean(weighted * middle, axis=-1, keepdims=True)
    middle_grad = upstream + scale * weighted - middle * scale * scale * scale * inner
    branch = middle_grad.astype(LOW)
    branch_ref[...] = branch
    for m in range(4):
        grad_refs[m][...] = dot_cols(branch, out_refs[m][...]).astype(LOW)


def backward_kernel(*refs):
    slot_ref, proj_ref, probs_ref, hits_ref = refs[:4]
    grad_refs = refs[4:8]
    pg_ref, table_ref, sums_ref = refs[8:11]
    width = grad_refs[0].shape[1]
    heads = width // HEAD_DIM
    slots = jnp.concatenate([ref[...] for ref in grad_refs], axis=0)
    grad = dot_rows(slot_hits(slot_ref[...], slots.shape[0]), slots).astype(LOW)
    query = proj_ref[:, :width]
    key = proj_ref[:, width : 2 * width]
    value = proj_ref[:, 2 * width : 3 * width]
    row = lax.broadcasted_iota(jnp.int32, (SEQ_LEN, SEQ_LEN), 0)
    col = lax.broadcasted_iota(jnp.int32, (SEQ_LEN, SEQ_LEN), 1)
    mirror = jnp.where(row + col == SEQ_LEN - 1, 1.0, 0.0).astype(LOW)
    zero = jnp.zeros((SEQ_LEN, width), WIDE)
    query_grad, key_grad, value_grad = zero, zero, zero
    sums_ref[...] = jnp.zeros_like(sums_ref)
    for h, mask in enumerate(head_masks(width)):
        probs_low = probs_ref[h]
        probs = probs_low.astype(WIDE)
        picked = grad * jnp.where(mask, 1.0, 0.0).astype(LOW)
        prob_grad = dot_cols(picked, value)
        inner = jnp.sum(probs * prob_grad, axis=-1, keepdims=True)
        score_grad = (probs * (prob_grad - inner)).astype(LOW)
        value_grad = jnp.where(mask, dot_rows(probs_low, grad), value_grad)
        key_grad = jnp.where(mask, dot_rows(score_grad, query), key_grad)
        query_grad = jnp.where(mask, dot_plain(score_grad, key), query_grad)
        mirrored = dot_rows(score_grad, mirror)
        wide = jnp.concatenate([mirrored, jnp.zeros((SEQ_LEN, SEQ_LEN), WIDE)], axis=1)
        turned = pltpu.roll(wide, 0, 1, stride=1, stride_axis=0)
        sums_ref[h : h + 1, :] = jnp.sum(turned, axis=0, keepdims=True)
    pg_ref[:, :width] = (query_grad * HEAD_DIM ** (-0.5)).astype(LOW)
    pg_ref[:, width : 2 * width] = (key_grad * HEAD_DIM ** (-0.5)).astype(LOW)
    pg_ref[:, 2 * width : 3 * width] = value_grad.astype(LOW)
    table_ref[...] = jnp.dot(sums_ref[...], hits_ref[...], precision=HIGH)


def weights_kernel(parts, place_ref, n_ref, pg_ref, *refs):
    mixed_refs, branch_refs, outs, total_ref = refs[:4], refs[4:8], refs[8:-1], refs[-1]
    width = mixed_refs[0].shape[1]
    total_ref[:, : 3 * width] = dot_rows(n_ref[...], pg_ref[...]).astype(LOW)
    mixed = jnp.concatenate([ref[...] for ref in mixed_refs], axis=0)
    branch = jnp.concatenate([ref[...] for ref in branch_refs], axis=0)
    total_ref[:, 3 * width :] = dot_rows(branch, mixed).astype(LOW)
    if parts == 1:
        outs[0][...] = total_ref[...]
    else:
        rows = D // parts
        for ref, half, order in zip(outs, (0, 0, 1, 1), FOLD_ORDERS):
            for at, m in enumerate(order):
                source = pl.multiple_of((place_ref[0] ^ m) * rows, rows)
                ref[at * rows : (at + 1) * rows, :] = total_ref[
                    pl.ds(source, rows), half * D // 2 : (half + 1) * D // 2
                ]


def fold_kernel(*refs):
    for at in range(2):
        keep_ref, came_ref = refs[2 * at : 2 * at + 2]
        kept_ref, sent_ref = refs[4 + 2 * at : 6 + 2 * at]
        rows = kept_ref.shape[0] // 2
        for block in range(4):
            here = slice(block * rows, (block + 1) * rows)
            to = slice(block // 2 * rows, (block // 2 + 1) * rows)
            total = keep_ref[here, :].astype(WIDE) + came_ref[here, :].astype(WIDE)
            if block % 2 == 0:
                kept_ref[to, :] = total
            else:
                sent_ref[to, :] = total.astype(LOW)


def last_fold_kernel(*refs):
    kept_ref, sent_ref = refs[4:]
    for at in range(2):
        keep_ref, came_ref = refs[2 * at : 2 * at + 2]
        rows, width = kept_ref.shape[0], keep_ref.shape[1]
        cols = slice(at * width, (at + 1) * width)
        total = keep_ref[...] + came_ref[...].astype(WIDE)
        kept_ref[:, cols] = total[:rows]
        sent_ref[:, cols] = total[rows:].astype(LOW)


def input_kernel(
    heads,
    place_ref,
    pg_ref,
    w_ref,
    x_ref,
    gain_ref,
    table_ref,
    early_ref,
    keep_ref,
    send_ref,
    wide_ref,
):
    tensor_place = place_ref[1]
    width = heads * HEAD_DIM
    wide_ref[...] = dot_cols(pg_ref[...], w_ref[:, : 3 * width])
    values = x_ref[...].astype(WIDE)
    scale = lax.rsqrt(jnp.mean(values * values, axis=-1, keepdims=True) + EPS_NORM)
    gain_grad = jnp.sum(wide_ref[...] * values * scale, axis=0, keepdims=True)
    quarter = SEQ_LEN // 4
    for half, distance in enumerate((0, 2)):
        near = pl.multiple_of((tensor_place ^ distance) * quarter, quarter)
        far = pl.multiple_of((tensor_place ^ distance ^ 1) * quarter, quarter)
        block = pl.ds(half * quarter, quarter)
        keep_ref[block, :] = wide_ref[pl.ds(near, quarter), :]
        send_ref[block, :] = wide_ref[pl.ds(far, quarter), :].astype(LOW)
    small = early_ref[...]
    line = lax.broadcasted_iota(jnp.int32, (small.shape[0], 1), 0)
    small = jnp.where(line == 0, gain_grad, small)
    for h in range(heads):
        counts = jnp.concatenate(
            [table_ref[h : h + 1, :], jnp.zeros((1, D - table_ref.shape[1]), WIDE)], axis=1
        )
        small = jnp.where(line == 1 + tensor_place * heads + h, counts, small)
    keep_ref[SEQ_LEN // 2 :, :] = small
    send_ref[SEQ_LEN // 2 :, :] = small.astype(LOW)


def update_kernel(*refs):
    came, weights, outs = refs[:-12], refs[-12:-6], refs[-6:]
    shard = weights[0].shape[1]
    total = jnp.zeros((shard, D), WIDE)
    for ref in came:
        for m in range(ref.shape[0] // shard):
            total = total + ref[m * shard : (m + 1) * shard, :].astype(WIDE)
    width = weights[0].shape[2]
    for c in range(3):
        grad = total[:, c * width : (c + 1) * width]
        made = adamw(*[ref[c] for ref in weights[:3]], grad, 3.0 * D ** (-0.5), DECAY)
        for ref, value in zip(outs[:3], made):
            ref[c] = value
    grad = jnp.transpose(total[:, 3 * width :])
    made = adamw(*[ref[...] for ref in weights[3:]], grad, 3.0 * FAN_O ** (-0.5), DECAY)
    for ref, value in zip(outs[3:], made):
        ref[...] = value


def gather_projections(own, ready, count):
    if count != 8:
        return [lax.all_gather(own, "expert", axis=0, tiled=True)], ready
    pieces = [own] + [None] * (count - 1)
    for m in range(count - 2, 0, -2):
        pieces[m] = swap(own, "expert", m)
    pieces[1] = swap(own, "expert", 1)
    pieces[2], ready = tie(pieces[2], ready)
    for m in range(2, count, 2):
        pieces[m + 1] = swap(pieces[m], "expert", 1)
    return pieces, ready


def body(
    block_input,
    cotangent,
    lengths,
    routes,
    norm_gains,
    gains_mean,
    gains_square,
    position_bias,
    bias_mean,
    bias_square,
    router,
    router_mean,
    router_square,
    qkv_weight,
    qkv_mean,
    qkv_square,
    out_weight,
    out_mean,
    out_square,
    expert_up,
    up_mean,
    up_square,
    expert_down,
    down_mean,
    down_square,
):
    tensor_size = lax.axis_size("tensor")
    tensor_place = lax.axis_index("tensor")
    expert_size = lax.axis_size("expert")
    place = lax.axis_index("expert")
    experts = expert_size // GROUP
    capacity = max(2, 9 * SEQ_LEN // (8 * expert_size))
    share = -(-capacity // tensor_size)
    own_slots = expert_size * share
    fan_down = max(1, FF // (experts * experts))
    heads_here = HEADS // tensor_size
    width = heads_here * HEAD_DIM
    rows_here = SEQ_LEN // tensor_size
    parts = expert_size if expert_size == 8 else 1
    shard = D // expert_size
    padded = -(-share // 8) * 8
    lines = -(-(2 + HEADS + experts) // 16) * 16
    scalars = jnp.stack([place, tensor_place]).astype(jnp.int32)

    own_shard = call(
        shard_kernel,
        [shape_of(LOW, shard, D)],
        [qkv_weight, out_weight],
        1,
        away=(0, 1),
        scratch=[
            pltpu.VMEM(qkv_weight.shape, WIDE),
            pltpu.VMEM(out_weight.shape, WIDE),
            pltpu.SemaphoreType.DMA((2,)),
        ],
    )[0]

    spread = np.zeros((expert_size, share, expert_size, padded), np.float32)
    for e in range(expert_size):
        spread[e, np.arange(share), e, np.arange(share)] = 1.0
    spread = jnp.asarray(spread.reshape(own_slots, expert_size * padded), LOW)
    offsets = np.arange(2 * SEQ_LEN)
    circular = np.where(offsets < SEQ_LEN, offsets, offsets - 2 * SEQ_LEN)
    circular_hits = jnp.asarray(offset_hits(circular, BUCKETS).T)
    half = expert_up.shape[1:]
    prepared = call(
        functools.partial(prepare_kernel, share),
        [
            shape_of(LOW, SEQ_LEN, D),
            shape_of(WIDE, heads_here, 2 * SEQ_LEN),
            shape_of(jnp.int32, 1, SEQ_LEN),
            shape_of(LOW, own_slots, D),
            shape_of(LOW, own_slots, D),
            shape_of(LOW, expert_size * padded, D),
            shape_of(LOW, *half),
            shape_of(LOW, *half),
        ],
        [
            scalars,
            routes.reshape(1, SEQ_LEN),
            norm_gains[0:1],
            spread,
            position_bias,
            circular_hits,
            block_input,
            cotangent,
            expert_up,
            expert_down,
        ],
        4,
        scalars=1,
        away=(6, 7, 8, 9),
        away_outs=(4, 6, 7),
        scratch=[
            pltpu.VMEM((SEQ_LEN, D), LOW),
            pltpu.VMEM((SEQ_LEN, D), LOW),
            pltpu.VMEM(expert_up.shape, WIDE),
            pltpu.VMEM(expert_up.shape, WIDE),
            pltpu.VMEM((own_slots, D), LOW),
            pltpu.VMEM(half, LOW),
            pltpu.VMEM(half, LOW),
            pltpu.SemaphoreType.DMA((7,)),
        ],
    )
    with jax.named_scope("cot_dispatch"):
        cot_came = exchange(prepared[5])
    prepared = prepared[:5] + prepared[6:]
    with jax.named_scope("projection_gather"):
        pieces, prepared = gather_projections(own_shard, prepared, expert_size)
    normed_one, offset_bias, slot_row, own_inputs, own_upstream, up_low, down_low = prepared
    joined = [shape_of(LOW, own_slots, D)]
    if parts > 1:
        down_low, pieces[6] = tie(down_low, pieces[6])
    with jax.named_scope("expert_gather"):
        down_far = swap(down_low, "expert", 2)
    projections, out_here = call(
        functools.partial(assemble_kernel, parts),
        [shape_of(LOW, D, D), shape_of(LOW, width, D)],
        [scalars] + pieces,
        1,
        scalars=1,
        scratch=[pltpu.SemaphoreType.DMA((parts,))],
        away=range(1, 1 + parts),
    )
    up_low, out_here = tie(up_low, out_here)
    with jax.named_scope("expert_gather"):
        up_near = swap(up_low, "expert", 1)
    with jax.named_scope("out_blocks"):
        out_blocks = tensor_blocks(out_here)
    projected, probs, *mixed_blocks = call(
        forward_kernel,
        [
            shape_of(LOW, SEQ_LEN, 3 * width),
            shape_of(LOW, heads_here, SEQ_LEN, SEQ_LEN),
        ]
        + [shape_of(LOW, own_slots, width)] * 4,
        [lengths, normed_one, offset_bias, slot_row, projections],
        6,
        scalars=1,
        away_outs=(0, 1),
        scratch=[
            pltpu.VMEM((SEQ_LEN, 3 * width), LOW),
            pltpu.VMEM((heads_here, SEQ_LEN, SEQ_LEN), LOW),
            pltpu.SemaphoreType.DMA((1 + heads_here,)),
        ],
    )
    router_rows = router.T

    mixed_blocks, up_near, down_far, cot_came = tie(mixed_blocks, up_near, down_far, cot_came)
    with jax.named_scope("expert_gather"):
        up_far = swap(jnp.concatenate([up_low, up_near], 0), "expert", 2)
        down_near = swap(jnp.concatenate([down_low, down_far], 0), "expert", 1)
    ups, downs = [up_low, up_near, up_far], [down_low, down_far, down_near]
    with jax.named_scope("mixed"):
        mixed_own = [mixed_blocks[0]] + [swap(mixed_blocks[m], "tensor", m) for m in range(1, 4)]
    own_cot = call(join_kernel, joined, [spread, cot_came], 1, limit=LIMIT_SMALL)[0]
    with jax.named_scope("cot_blocks"):
        grad_blocks = tensor_blocks(own_cot)

    middle, normed_two, rows_sent = call(
        middle_kernel,
        [
            shape_of(WIDE, own_slots, D),
            shape_of(LOW, own_slots, D),
            shape_of(LOW, expert_size * padded, D),
        ],
        [own_inputs, norm_gains[1:2], spread] + mixed_own + out_blocks,
        1,
    )
    with jax.named_scope("row_dispatch"):
        rows_came = exchange(rows_sent)
    own_rows = call(join_kernel, joined, [spread, rows_came], 1, limit=LIMIT_SMALL)[0]
    with jax.named_scope("row_blocks"):
        row_blocks = tensor_blocks(own_rows)

    hidden = 4 * expert_up.shape[1]
    rows_in, grad_rows, act, grad_pre, keep, send = call(
        expert_kernel,
        [
            shape_of(LOW, 4 * own_slots, D),
            shape_of(LOW, 4 * own_slots, D),
            shape_of(LOW, 4 * own_slots, hidden),
            shape_of(LOW, 4 * own_slots, hidden),
            shape_of(WIDE, 2 * own_slots, 2 * D),
            shape_of(LOW, 2 * own_slots, 2 * D),
        ],
        [scalars, router_rows] + row_blocks + grad_blocks + ups + downs,
        8,
        scalars=1,
        limit=LIMIT_SMALL,
    )
    half_up = shape_of(WIDE, hidden // 2, D)
    sent_up = shape_of(LOW, hidden // 2, D)
    up_keep, up_send, down_keep, down_send = call(
        expert_weights_kernel,
        [half_up, sent_up, half_up, sent_up],
        [rows_in, grad_rows, act, grad_pre],
        3,
        limit=LIMIT_SMALL,
    )
    with jax.named_scope("return_sum"):
        came = swap(send, "tensor", 1)
    came, up_send, down_send = tie(came, up_send, down_send)
    with jax.named_scope("expert_reduce"):
        up_came = swap(up_send, "expert", 2)
        down_came = swap(down_send, "expert", 1)
    kept, send = call(
        half_kernel,
        [shape_of(WIDE, own_slots, 2 * D), shape_of(LOW, own_slots, 2 * D)],
        [keep, came],
        1,
        limit=LIMIT_SMALL,
    )
    with jax.named_scope("return_sum"):
        came = swap(send, "tensor", 2)
    sent = call(
        spread_kernel,
        [shape_of(LOW, expert_size * padded, 2 * D)],
        [kept, came, spread],
        1,
        limit=LIMIT_SMALL,
    )[0]
    sent, up_came, down_came = tie(sent, up_came, down_came)
    with jax.named_scope("row_return"):
        returned = exchange(sent)
    quarter = (hidden // 4, D)
    up_half, up_send, down_half, down_send = call(
        reduce_kernel,
        [shape_of(WIDE, *quarter), shape_of(LOW, *quarter)] * 2,
        [up_keep, up_came, down_keep, down_came],
        1,
        limit=LIMIT_SMALL,
    )
    with jax.named_scope("expert_reduce"):
        up_last = swap(up_send, "expert", 1)
        down_last = swap(down_send, "expert", 2)

    branch_grad, block_slots, early, *mixed_grads = call(
        functools.partial(after_kernel, share),
        [
            shape_of(LOW, own_slots, D),
            shape_of(LOW, own_slots, D),
            shape_of(WIDE, lines, D),
        ]
        + [shape_of(LOW, own_slots, width)] * 4,
        [middle, normed_two, own_upstream, norm_gains[1:2], router_rows, spread, returned]
        + out_blocks,
        4,
    )
    with jax.named_scope("mixed_grad"):
        mixed_grads = [mixed_grads[0]] + [swap(mixed_grads[m], "tensor", m) for m in range(1, 4)]
    mixed_grads, branch_grad, up_last, down_last = tie(
        mixed_grads, branch_grad, up_last, down_last
    )
    with jax.named_scope("branch_blocks"):
        branch_far = swap(branch_grad, "tensor", 2)
        branch_near = swap(branch_grad, "tensor", 1)
    mirrored = np.arange(2 * SEQ_LEN) - (SEQ_LEN - 1)
    projected_grad, table_grad, _ = call(
        backward_kernel,
        [
            shape_of(LOW, SEQ_LEN, 3 * width),
            shape_of(WIDE, 8, 128),
            shape_of(WIDE, 8, 2 * SEQ_LEN),
        ],
        [slot_row, projected, probs, jnp.asarray(offset_hits(mirrored, 128))] + mixed_grads,
        5,
    )
    branch_far, projected_grad = tie(branch_far, projected_grad)
    with jax.named_scope("branch_blocks"):
        branch_both = swap(branch_far, "tensor", 1)
    branch_blocks = [branch_grad, branch_near, branch_far, branch_both]
    grad_sent = call(
        functools.partial(weights_kernel, parts),
        [shape_of(LOW, D, D)] if parts == 1 else [shape_of(LOW, D // 2, D // 2)] * 4,
        [scalars, normed_one, projected_grad] + list(mixed_blocks) + branch_blocks,
        2,
        limit=LIMIT_SMALL,
        scalars=1,
        scratch=[pltpu.VMEM((D, D), LOW)],
    )
    grad_sent, projected_grad = tie(grad_sent, projected_grad)
    with jax.named_scope("projection_reduce"):
        if parts == 1:
            grad_came = [exchange(grad_sent[0])]
        else:
            one_keep, one_sent, two_keep, two_sent = grad_sent
            one_came, two_came = swap(one_sent, "expert", 1), swap(two_sent, "expert", 2)
    keep, send = call(
        functools.partial(input_kernel, heads_here),
        [
            shape_of(WIDE, 2 * rows_here + lines, D),
            shape_of(LOW, 2 * rows_here + lines, D),
        ],
        [
            scalars,
            projected_grad,
            projections,
            block_input,
            norm_gains[0:1],
            table_grad,
            early,
        ],
        2,
        limit=LIMIT_SMALL,
        scalars=1,
        scratch=[pltpu.VMEM((SEQ_LEN, D), WIDE)],
    )
    with jax.named_scope("input_sum"):
        came = swap(send, "tensor", 1)
    came, up_half, down_half = tie(came, up_half, down_half)
    kept, send = call(
        input_half_kernel,
        [shape_of(WIDE, rows_here + lines, D), shape_of(LOW, rows_here + lines, D)],
        [keep, came],
        1,
        limit=LIMIT_SMALL,
    )
    state = pltpu.VMEM(expert_up.shape, WIDE)
    (
        new_up_mean,
        new_up_square,
        new_expert_up,
        new_down_mean,
        new_down_square,
        new_expert_down,
    ) = call(
        functools.partial(
            expert_update_kernel, (3.0 * D ** (-0.5), 3.0 * fan_down ** (-0.5))
        ),
        [shape_of(WIDE, *expert_up.shape)] * 6,
        [
            up_half,
            up_last,
            down_half,
            down_last,
            expert_up,
            up_mean,
            up_square,
            expert_down,
            down_mean,
            down_square,
        ],
        4,
        away=range(4, 10),
        away_outs=range(6),
        scratch=[state] * 12 + [pltpu.SemaphoreType.DMA((12,))],
    )
    if parts > 1:
        one_came, send, new_up_mean = tie(one_came, send, new_up_mean)
    with jax.named_scope("projection_reduce"):
        if parts > 1:
            one_came, block_slots = tie(one_came, block_slots)
            one_keep, one_sent, two_keep, two_sent = call(
                fold_kernel,
                [shape_of(WIDE, D // 4, D // 2), shape_of(LOW, D // 4, D // 2)] * 2,
                [one_keep, one_came, two_keep, two_came],
                1,
                limit=LIMIT_SMALL,
            )
            one_came, two_came = swap(one_sent, "expert", 2), swap(two_sent, "expert", 1)
            grad_kept, sent = call(
                last_fold_kernel,
                [shape_of(WIDE, shard, D), shape_of(LOW, shard, D)],
                [one_keep, one_came, two_keep, two_came],
                1,
                limit=LIMIT_SMALL,
            )
            grad_came = [grad_kept, swap(sent, "expert", 4)]
    with jax.named_scope("input_sum"):
        came = swap(send, "tensor", 2)
        small = kept[rows_here:] + came[rows_here:].astype(WIDE)
        grad_came, came = tie(grad_came, came)
        normed_one_grad = kept[:rows_here] + came[:rows_here].astype(WIDE)
    with jax.named_scope("block_blocks"):
        block_blocks = tensor_blocks(block_slots)

    with jax.named_scope("small_sum"):
        small = exchange(jnp.tile(small.astype(LOW), (expert_size, 1))).astype(WIDE)
        small = jnp.sum(small.reshape(expert_size, lines, D), axis=0)
    own_start = tensor_place * rows_here
    slot_own = lax.dynamic_slice_in_dim(slot_row[0], own_start, rows_here, 0)
    own_hits = (
        slot_own[:, None] == jnp.arange(tensor_size * own_slots, dtype=jnp.int32)[None, :]
    ).astype(LOW)
    block_output = dot_plain(own_hits, jnp.concatenate(block_blocks, 0)).astype(LOW)
    middle_own = dot_plain(own_hits, jnp.concatenate(branch_blocks, 0))
    inputs_own = lax.dynamic_slice_in_dim(block_input, own_start, rows_here, 0).astype(WIDE)
    scale_own = lax.rsqrt(jnp.mean(inputs_own * inputs_own, axis=-1, keepdims=True) + EPS_NORM)
    weighted = normed_one_grad * norm_gains[0]
    inner = jnp.mean(weighted * inputs_own, axis=-1, keepdims=True)
    input_grad = (
        middle_own
        + scale_own * weighted
        - inputs_own * scale_own * scale_own * scale_own * inner
    )

    gains_grad = jnp.concatenate([small[0:1], small[1 + HEADS : 2 + HEADS]], 0)
    bias_grad = small[1 : 1 + HEADS, :BUCKETS].T
    router_grad = small[2 + HEADS : 2 + HEADS + experts].T

    new_gains_mean, new_gains_square, new_norm_gains = adamw(
        norm_gains, gains_mean, gains_square, gains_grad, 0.3, 0.0
    )
    new_bias_mean, new_bias_square, new_position_bias = adamw(
        position_bias, bias_mean, bias_square, bias_grad, 1.5, 0.0
    )
    new_router_mean, new_router_square, new_router = adamw(
        router, router_mean, router_square, router_grad, 3.0 * (2 * D) ** (-0.5), DECAY
    )
    new_qkv_mean, new_qkv_square, new_qkv_weight, new_out_mean, new_out_square, new_out_weight = (
        call(
            update_kernel,
            [shape_of(WIDE, *qkv_weight.shape)] * 3 + [shape_of(WIDE, *out_weight.shape)] * 3,
            grad_came
            + [
                qkv_weight,
                qkv_mean,
                qkv_square,
                out_weight,
                out_mean,
                out_square,
            ],
            40,
            )
    )
    return (
        block_output,
        input_grad,
        new_gains_mean,
        new_gains_square,
        new_norm_gains,
        new_bias_mean,
        new_bias_square,
        new_position_bias,
        new_router_mean,
        new_router_square,
        new_router,
        new_qkv_mean,
        new_qkv_square,
        new_qkv_weight,
        new_out_mean,
        new_out_square,
        new_out_weight,
        new_up_mean,
        new_up_square,
        new_expert_up,
        new_down_mean,
        new_down_square,
        new_expert_down,
    )


def solution(mesh):
    return jax.shard_map(
        body,
        mesh=mesh,
        in_specs=(
            P("expert", None),
            P("expert", None),
            P("expert"),
            P("expert", None),
            P(),
            P(),
            P(),
            P(),
            P(),
            P(),
            P(),
            P(),
            P(),
            P(None, "expert", "tensor"),
            P(None, "expert", "tensor"),
            P(None, "expert", "tensor"),
            P("tensor", "expert"),
            P("tensor", "expert"),
            P("tensor", "expert"),
            P("expert", "tensor", None),
            P("expert", "tensor", None),
            P("expert", "tensor", None),
            P("expert", "tensor", None),
            P("expert", "tensor", None),
            P("expert", "tensor", None),
        ),
        out_specs=(
            P(("expert", "tensor"), None),
            P(("expert", "tensor"), None),
            P(),
            P(),
            P(),
            P(),
            P(),
            P(),
            P(),
            P(),
            P(),
            P(None, "expert", "tensor"),
            P(None, "expert", "tensor"),
            P(None, "expert", "tensor"),
            P("tensor", "expert"),
            P("tensor", "expert"),
            P("tensor", "expert"),
            P("expert", "tensor", None),
            P("expert", "tensor", None),
            P("expert", "tensor", None),
            P("expert", "tensor", None),
            P("expert", "tensor", None),
            P("expert", "tensor", None),
        ),
        check_vma=False,
    )
```

```python
import functools

import jax
import jax.numpy as jnp
import numpy as np
from jax import lax
from jax.experimental import pallas as pl
from jax.experimental.pallas import tpu as pltpu
from jax.sharding import PartitionSpec as P

D = 768
HEADS = 12
HEAD_DIM = 64
FF = 3072
BUCKETS = 32
MAX_DIST = 128
GROUP = 4
STEP = 10
SEQ_LEN = 512
FAN_O = 3


EPS_NORM = 1e-06
BETA_ONE = 0.9
BETA_TWO = 0.999
EPS_ADAM = 1e-08
DECAY = 0.01
MASKED = -1e30
HIGH = lax.Precision.HIGHEST
LIMIT_SMALL = 40 * 2**20
LIMIT_LARGE = 56 * 2**20
LOW = jnp.bfloat16
WIDE = jnp.float32


FOLD_ORDERS = ((0, 2, 4, 6), (1, 3, 5, 7), (0, 1, 4, 5), (2, 3, 6, 7))


def tie(*groups):
    return lax.optimization_barrier(groups)


def swap(block, axis, distance):
    count = lax.axis_size(axis)
    return lax.ppermute(block, axis, [(low, low ^ distance) for low in range(count)])


def exchange(rows):
    return lax.all_to_all(rows, "expert", split_axis=0, concat_axis=0, tiled=True)


def tensor_blocks(block):
    far = swap(block, "tensor", 2)
    near = swap(block, "tensor", 1)
    return [block, near, far, swap(far, "tensor", 1)]


def bucket_of(offset):
    half = BUCKETS // 2
    exact = half // 2
    distance = np.abs(offset)
    far = np.full(offset.shape, exact, np.int32)
    for level in range(exact + 1, half):
        limit = int(
            np.ceil(exact * (MAX_DIST / exact) ** ((level - exact) / (half - exact)) - 1e-09)
        )
        far = far + (distance >= limit)
    return np.where(offset > 0, half, 0) + np.where(distance < exact, distance, far)


def offset_hits(offsets, width):
    hits = (bucket_of(offsets)[:, None] == np.arange(width)[None, :]) & (
        np.abs(offsets)[:, None] < SEQ_LEN
    )
    return hits.astype(np.float32)


def adamw(weight, mean, square, grad, rate, decay):
    mean_new = BETA_ONE * mean + (1.0 - BETA_ONE) * grad
    square_new = BETA_TWO * square + (1.0 - BETA_TWO) * grad * grad
    mean_hat = mean_new / (1.0 - BETA_ONE**STEP)
    square_hat = square_new / (1.0 - BETA_TWO**STEP)
    weight_new = weight - rate * (mean_hat / (jnp.sqrt(square_hat) + EPS_ADAM) + decay * weight)
    return (mean_new, square_new, weight_new)


def dot_rows(left, right):
    return lax.dot_general(left, right, (((0,), (0,)), ((), ())), preferred_element_type=WIDE)


def dot_cols(left, right):
    return lax.dot_general(left, right, (((1,), (1,)), ((), ())), preferred_element_type=WIDE)


def dot_plain(left, right):
    return jnp.dot(left, right, preferred_element_type=WIDE)


def call(
    kernel, outs, operands, micros, scalars=0, scratch=(), away=(), away_outs=(), limit=LIMIT_LARGE
):
    vmem = pl.BlockSpec(memory_space=pltpu.VMEM)
    hbm = pl.BlockSpec(memory_space=pltpu.HBM)
    smem = pl.BlockSpec(memory_space=pltpu.SMEM)
    return pl.pallas_call(
        kernel,
        out_shape=outs,
        in_specs=[
            smem if at < scalars else hbm if at in away else vmem for at in range(len(operands))
        ],
        out_specs=[hbm if at in away_outs else vmem for at in range(len(outs))],
        scratch_shapes=list(scratch),
        compiler_params=pltpu.CompilerParams(vmem_limit_bytes=limit),
        cost_estimate=pl.CostEstimate(
            flops=int(micros * 9e8), bytes_accessed=0, transcendentals=0
        ),
    )(*operands)


def start_copies(sources, targets, sems, first=0):
    copies = [
        pltpu.make_async_copy(source, target, sems.at[first + at])
        for at, (source, target) in enumerate(zip(sources, targets))
    ]
    for copy in copies:
        copy.start()
    return copies


def wait_copies(copies):
    for copy in copies:
        copy.wait()


def shape_of(dtype, *sizes):
    return jax.ShapeDtypeStruct(sizes, dtype)


def head_masks(width):
    lane = lax.broadcasted_iota(jnp.int32, (1, width), 1)
    return [
        (lane >= h * HEAD_DIM) & (lane < (h + 1) * HEAD_DIM) for h in range(width // HEAD_DIM)
    ]


def slot_hits(slot_row, count):
    slots = lax.broadcasted_iota(jnp.int32, (count, slot_row.shape[1]), 0)
    return jnp.where(slots == slot_row, 1.0, 0.0).astype(LOW)


def shard_kernel(qkv_far, out_far, shard_ref, qkv_ref, out_ref, sems):
    wait_copies(start_copies([qkv_far, out_far], [qkv_ref, out_ref], sems))
    width = qkv_ref.shape[2]
    for c in range(3):
        shard_ref[:, c * width : (c + 1) * width] = qkv_ref[c].astype(LOW)
    row = lax.broadcasted_iota(jnp.int32, (width, width), 0)
    col = lax.broadcasted_iota(jnp.int32, (width, width), 1)
    same = jnp.where(row == col, 1.0, 0.0).astype(LOW)
    shard_ref[:, 3 * width :] = dot_rows(out_ref[...].astype(LOW), same).astype(LOW)


def prepare_kernel(
    share,
    place_ref,
    target_ref,
    gain_ref,
    spread_ref,
    bias_ref,
    circular_ref,
    x_far,
    cot_far,
    up_far,
    down_far,
    n_ref,
    offset_ref,
    slot_ref,
    xs_ref,
    cs_far,
    cot_out_ref,
    up_out,
    down_out,
    x_ref,
    cot_ref,
    up_ref,
    down_ref,
    cs_ref,
    up_low_ref,
    down_low_ref,
    sems,
):
    first = start_copies([x_far, cot_far], [x_ref, cot_ref], sems)
    second = start_copies([up_far, down_far], [up_ref, down_ref], sems, 2)
    own_slots = xs_ref.shape[0]
    target = target_ref[...]
    replica = lax.broadcasted_iota(jnp.int32, (own_slots // share, SEQ_LEN), 0)
    named = jnp.where(replica == target, 1.0, 0.0)
    row = lax.broadcasted_iota(jnp.int32, (SEQ_LEN, SEQ_LEN), 0)
    col = lax.broadcasted_iota(jnp.int32, (SEQ_LEN, SEQ_LEN), 1)
    upto = jnp.where(row < col, 1.0, 0.0).astype(LOW)
    ranks = dot_plain(named.astype(LOW), upto)
    rank = jnp.sum(named * ranks, axis=0, keepdims=True).astype(jnp.int32)
    owner = jnp.zeros_like(rank)
    for m in range(1, 4):
        owner = owner + jnp.where(rank >= m * share, 1, 0)
    slot = (owner ^ place_ref[1]) * own_slots + target * share + rank - owner * share
    slot_ref[...] = slot
    hits = slot_hits(slot, own_slots)
    wait_copies(first)
    xs_ref[...] = dot_plain(hits, x_ref[...]).astype(LOW)
    own = dot_plain(hits, cot_ref[...]).astype(LOW)
    cs_ref[...] = own
    cot_out_ref[...] = dot_rows(spread_ref[...], own).astype(LOW)
    third = start_copies([cs_ref], [cs_far], sems, 4)
    values = x_ref[...].astype(WIDE)
    scale = lax.rsqrt(jnp.mean(values * values, axis=-1, keepdims=True) + EPS_NORM)
    n_ref[...] = (values * scale * gain_ref[...]).astype(LOW)
    heads = lax.dot_general(
        bias_ref[...],
        circular_ref[...],
        (((0,), (0,)), ((), ())),
        precision=HIGH,
        preferred_element_type=WIDE,
    )
    for h in range(offset_ref.shape[0]):
        row = lax.broadcasted_iota(jnp.int32, (heads.shape[0], 1), 0)
        here = row == place_ref[1] * offset_ref.shape[0] + h
        offset_ref[h : h + 1, :] = jnp.sum(jnp.where(here, heads, 0.0), axis=0, keepdims=True)
    wait_copies(second)
    up_low_ref[...] = up_ref[0].astype(LOW)
    down_low_ref[...] = down_ref[0].astype(LOW)
    wait_copies(third + start_copies([up_low_ref, down_low_ref], [up_out, down_out], sems, 5))


def assemble_kernel(parts, place_ref, *refs):
    pieces = refs[:parts]
    w_ref, out_ref, sems = refs[parts:]
    rows = D // parts
    copies = []
    for m in range(parts):
        at = pl.multiple_of((place_ref[0] ^ m) * rows, rows) if parts > 1 else 0
        copy = pltpu.make_async_copy(pieces[m], w_ref.at[pl.ds(at, rows), :], sems.at[m])
        copy.start()
        copies.append(copy)
    for copy in copies:
        copy.wait()
    width = out_ref.shape[0]
    row = lax.broadcasted_iota(jnp.int32, (width, width), 0)
    col = lax.broadcasted_iota(jnp.int32, (width, width), 1)
    same = jnp.where(row == col, 1.0, 0.0).astype(LOW)
    out_ref[...] = dot_cols(same, w_ref[:, 3 * width :]).astype(LOW)


def forward_kernel(length_ref, n_ref, offset_ref, slot_ref, w_ref, *refs):
    proj_far, probs_far = refs[:2]
    mixed_refs = refs[2:6]
    proj_ref, probs_ref, sems = refs[6:]
    width = mixed_refs[0].shape[1]
    proj_ref[...] = dot_plain(n_ref[...], w_ref[:, : 3 * width]).astype(LOW)
    copies = start_copies([proj_ref], [proj_far], sems)
    query = proj_ref[:, :width]
    key = proj_ref[:, width : 2 * width]
    value = proj_ref[:, 2 * width : 3 * width]
    live = lax.broadcasted_iota(jnp.int32, (1, SEQ_LEN), 1) < length_ref[0]
    mixed = jnp.zeros((SEQ_LEN, width), WIDE)
    for h, mask in enumerate(head_masks(width)):
        picked = query * jnp.where(mask, 1.0, 0.0).astype(LOW)
        line = jnp.broadcast_to(offset_ref[h : h + 1, :], (SEQ_LEN, 2 * SEQ_LEN))
        bias = pltpu.roll(line, 0, 1, stride=1, stride_axis=0)[:, :SEQ_LEN]
        scores = dot_cols(picked, key) * HEAD_DIM ** (-0.5) + bias
        scores = jnp.where(live, scores, MASKED)
        expo = jnp.exp(scores - jnp.max(scores, axis=-1, keepdims=True))
        probs = expo * (1.0 / jnp.sum(expo, axis=-1, keepdims=True))
        probs_ref[h] = probs.astype(LOW)
        copies += start_copies([probs_ref.at[h]], [probs_far.at[h]], sems, 1 + h)
        mixed = jnp.where(mask, dot_plain(probs_ref[h], value), mixed)
    count = mixed_refs[0].shape[0]
    hits = slot_hits(slot_ref[...], 4 * count)
    slots = dot_plain(hits, mixed.astype(LOW)).astype(LOW)
    for m in range(4):
        mixed_refs[m][...] = slots[m * count : (m + 1) * count, :]
    wait_copies(copies)


def join_kernel(spread_ref, came_ref, rows_ref):
    rows_ref[...] = dot_plain(spread_ref[...], came_ref[...]).astype(LOW)


def route_probs(rows, router_ref):
    logits = lax.dot_general(
        rows.astype(WIDE),
        router_ref[...],
        (((1,), (1,)), ((), ())),
        precision=HIGH,
        preferred_element_type=WIDE,
    )
    expo = jnp.exp(logits - jnp.max(logits, axis=-1, keepdims=True))
    return expo / jnp.sum(expo, axis=-1, keepdims=True)


def middle_kernel(x_ref, gain_ref, spread_ref, *refs):
    mixed_refs, out_refs = refs[:4], refs[4:8]
    middle_ref, normed_ref, sent_ref = refs[8:]
    middle = x_ref[...].astype(WIDE)
    for m in range(4):
        middle = middle + dot_plain(mixed_refs[m][...], out_refs[m][...])
    middle_ref[...] = middle
    scale = lax.rsqrt(jnp.mean(middle * middle, axis=-1, keepdims=True) + EPS_NORM)
    normed = (middle * scale * gain_ref[...]).astype(LOW)
    normed_ref[...] = normed
    sent_ref[...] = dot_rows(spread_ref[...], normed).astype(LOW)


def expert_kernel(*refs):
    place_ref, router_ref = refs[:2]
    row_refs, cot_refs = refs[2:6], refs[6:10]
    up_refs, down_refs = refs[10:13], refs[13:16]
    rows_ref, grads_ref, act_ref, pre_grad_ref = refs[16:20]
    keep_ref, send_ref = refs[20:22]
    weight_up = jnp.concatenate([ref[...] for ref in up_refs], axis=0)
    near, far, pair = down_refs
    shard = near.shape[0]
    weight_down = jnp.concatenate([near[...], pair[:shard, :], far[...], pair[shard:, :]], axis=0)
    count = row_refs[0].shape[0]
    for at, m in enumerate((0, 2, 1, 3)):
        rows_ref[at * count : (at + 1) * count, :] = row_refs[m][...]
        grads_ref[at * count : (at + 1) * count, :] = cot_refs[m][...]
    rows = rows_ref[...]
    probs = route_probs(rows, router_ref)
    here = lax.broadcasted_iota(jnp.int32, (1, probs.shape[1]), 1) == place_ref[0] // GROUP
    gate = jnp.sum(jnp.where(here, probs, 0.0), axis=-1, keepdims=True)
    grads_ref[...] = (gate * grads_ref[...].astype(WIDE)).astype(LOW)
    pre = dot_cols(rows, weight_up)
    root = np.sqrt(2 / np.pi).astype(np.float32)
    bend = np.float32(0.044715)
    square = pre * pre
    curve = jnp.tanh(root * (pre + bend * square * pre))
    act_ref[...] = (0.5 * pre * (1.0 + curve)).astype(LOW)
    slope = 0.5 * (1.0 + curve) + 0.5 * pre * (1.0 - curve * curve) * root * (
        1.0 + 3.0 * bend * square
    )
    pre_grad_ref[...] = (slope * dot_cols(grads_ref[...], weight_down)).astype(LOW)
    out = dot_plain(act_ref[...], weight_down)
    back = dot_plain(pre_grad_ref[...], weight_up)
    keep_ref[:, :D] = out[: 2 * count]
    keep_ref[:, D:] = back[: 2 * count]
    send_ref[:, :D] = out[2 * count :].astype(LOW)
    send_ref[:, D:] = back[2 * count :].astype(LOW)


def reduce_kernel(*refs):
    for at in range(2):
        keep_ref, came_ref = refs[2 * at : 2 * at + 2]
        half_ref, sent_ref = refs[4 + 2 * at : 6 + 2 * at]
        rows = half_ref.shape[0]
        half_ref[...] = keep_ref[:rows, :] + came_ref[:rows, :].astype(WIDE)
        sent_ref[...] = (keep_ref[rows:, :] + came_ref[rows:, :].astype(WIDE)).astype(LOW)


def expert_update_kernel(rates, up_half_ref, up_last_ref, down_half_ref, down_last_ref, *refs):
    sources, results, held, made, sems = refs[:6], refs[6:12], refs[12:18], refs[18:24], refs[24]
    first = start_copies(sources[:3], held[:3], sems)
    second = start_copies(sources[3:], held[3:], sems, 3)
    copies = []
    for at, (half_ref, last_ref, fetched) in enumerate(
        ((up_half_ref, up_last_ref, first), (down_half_ref, down_last_ref, second))
    ):
        wait_copies(fetched)
        grad = half_ref[...] + last_ref[...].astype(WIDE)
        here = slice(3 * at, 3 * at + 3)
        values = adamw(*[ref[0] for ref in held[here]], grad, rates[at], DECAY)
        for ref, value in zip(made[here], values):
            ref[0] = value
        copies += start_copies(made[here], results[here], sems, 6 + 3 * at)
    wait_copies(copies)


def input_half_kernel(place_ref, keep_ref, came_ref, slot_ref, *refs):
    branch_refs = refs[:4]
    kept_ref, sent_ref, middle_ref = refs[4:]
    rows = SEQ_LEN // 4
    own = slot_ref[:, pl.ds(pl.multiple_of(place_ref[1] * rows, rows), rows)]
    branch = jnp.concatenate([ref[...] for ref in branch_refs], axis=0)
    middle_ref[...] = dot_rows(slot_hits(own, branch.shape[0]), branch)
    kept_ref[:rows, :] = keep_ref[:rows, :] + came_ref[:rows, :].astype(WIDE)
    kept_ref[rows:, :] = keep_ref[2 * rows :, :] + came_ref[2 * rows :, :].astype(WIDE)
    far = keep_ref[rows : 2 * rows, :] + came_ref[rows : 2 * rows, :].astype(WIDE)
    sent_ref[:rows, :] = far.astype(LOW)
    sent_ref[rows:, :] = kept_ref[rows:, :].astype(LOW)


def half_kernel(keep_ref, came_ref, kept_ref, sent_ref):
    rows = kept_ref.shape[0]
    kept_ref[...] = keep_ref[:rows, :] + came_ref[:rows, :].astype(WIDE)
    sent_ref[...] = (keep_ref[rows:, :] + came_ref[rows:, :].astype(WIDE)).astype(LOW)


def spread_kernel(kept_ref, came_ref, spread_ref, sent_ref):
    whole = (kept_ref[...] + came_ref[...].astype(WIDE)).astype(LOW)
    sent_ref[...] = dot_rows(spread_ref[...], whole).astype(LOW)


def expert_weights_kernel(rows_ref, grads_ref, act_ref, pre_grad_ref, *outs):
    up_keep_ref, up_send_ref, down_keep_ref, down_send_ref = outs
    up = dot_rows(pre_grad_ref[...], rows_ref[...])
    down = dot_rows(act_ref[...], grads_ref[...])
    rows = up.shape[0] // 4
    up_keep_ref[...] = up[: 2 * rows]
    up_send_ref[...] = up[2 * rows :].astype(LOW)
    down_keep_ref[:rows, :] = down[:rows]
    down_keep_ref[rows:, :] = down[2 * rows : 3 * rows]
    down_send_ref[:rows, :] = down[rows : 2 * rows].astype(LOW)
    down_send_ref[rows:, :] = down[3 * rows :].astype(LOW)


def after_kernel(share, *refs):
    middle_ref, normed_ref, cot_ref, gain_ref, router_ref, spread_ref, came_ref = refs[:7]
    out_refs = refs[7:11]
    branch_ref, block_ref, small_ref = refs[11:14]
    grad_refs = refs[14:]
    returned = dot_plain(spread_ref[...], came_ref[...])
    expert_out, routed_grad = returned[:, :D], returned[:, D:]
    middle = middle_ref[...]
    scale = lax.rsqrt(jnp.mean(middle * middle, axis=-1, keepdims=True) + EPS_NORM)
    probs = route_probs(normed_ref[...], router_ref)
    count, experts = probs.shape
    row = lax.broadcasted_iota(jnp.int32, (count, experts), 0)
    col = lax.broadcasted_iota(jnp.int32, (count, experts), 1)
    chosen = jnp.zeros((count, experts), WIDE)
    for m in range(count // share):
        inside = (row >= m * share) & (row < (m + 1) * share)
        chosen = jnp.where(inside & (col == m // GROUP), 1.0, chosen)
    gate = jnp.sum(chosen * probs, axis=-1, keepdims=True)
    upstream = cot_ref[...].astype(WIDE)
    block_ref[...] = (middle + gate * expert_out).astype(LOW)
    gate_grad = jnp.sum(upstream * expert_out, axis=-1, keepdims=True)
    logit_grad = gate * (chosen - probs) * gate_grad
    router_term = jnp.dot(
        logit_grad, router_ref[...], precision=HIGH, preferred_element_type=WIDE
    )
    router_grad = lax.dot_general(
        logit_grad,
        normed_ref[...].astype(WIDE),
        (((0,), (0,)), ((), ())),
        precision=HIGH,
        preferred_element_type=WIDE,
    )
    normed_grad = routed_grad + router_term
    small_ref[...] = jnp.zeros_like(small_ref)
    small_ref[1 + HEADS : 2 + HEADS, :] = jnp.sum(
        normed_grad * middle * scale, axis=0, keepdims=True
    )
    small_ref[2 + HEADS : 2 + HEADS + experts, :] = router_grad
    weighted = normed_grad * gain_ref[...]
    inner = jnp.mean(weighted * middle, axis=-1, keepdims=True)
    middle_grad = upstream + scale * weighted - middle * scale * scale * scale * inner
    branch = middle_grad.astype(LOW)
    branch_ref[...] = branch
    for m in range(4):
        grad_refs[m][...] = dot_cols(branch, out_refs[m][...]).astype(LOW)


def backward_kernel(*refs):
    slot_ref, proj_ref, probs_ref, hits_ref = refs[:4]
    grad_refs = refs[4:8]
    pg_ref, table_ref, sums_ref = refs[8:11]
    width = grad_refs[0].shape[1]
    heads = width // HEAD_DIM
    slots = jnp.concatenate([ref[...] for ref in grad_refs], axis=0)
    grad = dot_rows(slot_hits(slot_ref[...], slots.shape[0]), slots).astype(LOW)
    query = proj_ref[:, :width]
    key = proj_ref[:, width : 2 * width]
    value = proj_ref[:, 2 * width : 3 * width]
    row = lax.broadcasted_iota(jnp.int32, (SEQ_LEN, SEQ_LEN), 0)
    col = lax.broadcasted_iota(jnp.int32, (SEQ_LEN, SEQ_LEN), 1)
    mirror = jnp.where(row + col == SEQ_LEN - 1, 1.0, 0.0).astype(LOW)
    zero = jnp.zeros((SEQ_LEN, width), WIDE)
    query_grad, key_grad, value_grad = zero, zero, zero
    sums_ref[...] = jnp.zeros_like(sums_ref)
    for h, mask in enumerate(head_masks(width)):
        probs_low = probs_ref[h]
        probs = probs_low.astype(WIDE)
        picked = grad * jnp.where(mask, 1.0, 0.0).astype(LOW)
        prob_grad = dot_cols(picked, value)
        inner = jnp.sum(probs * prob_grad, axis=-1, keepdims=True)
        score_grad = (probs * (prob_grad - inner)).astype(LOW)
        value_grad = jnp.where(mask, dot_rows(probs_low, grad), value_grad)
        key_grad = jnp.where(mask, dot_rows(score_grad, query), key_grad)
        query_grad = jnp.where(mask, dot_plain(score_grad, key), query_grad)
        mirrored = dot_rows(score_grad, mirror)
        wide = jnp.concatenate([mirrored, jnp.zeros((SEQ_LEN, SEQ_LEN), WIDE)], axis=1)
        turned = pltpu.roll(wide, 0, 1, stride=1, stride_axis=0)
        sums_ref[h : h + 1, :] = jnp.sum(turned, axis=0, keepdims=True)
    pg_ref[:, :width] = (query_grad * HEAD_DIM ** (-0.5)).astype(LOW)
    pg_ref[:, width : 2 * width] = (key_grad * HEAD_DIM ** (-0.5)).astype(LOW)
    pg_ref[:, 2 * width : 3 * width] = value_grad.astype(LOW)
    table_ref[...] = jnp.dot(sums_ref[...], hits_ref[...], precision=HIGH)


def weights_kernel(parts, place_ref, n_ref, pg_ref, *refs):
    mixed_refs, branch_refs, outs, total_ref = refs[:4], refs[4:8], refs[8:-1], refs[-1]
    width = mixed_refs[0].shape[1]
    total_ref[:, : 3 * width] = dot_rows(n_ref[...], pg_ref[...]).astype(LOW)
    mixed = jnp.concatenate([ref[...] for ref in mixed_refs], axis=0)
    branch = jnp.concatenate([ref[...] for ref in branch_refs], axis=0)
    total_ref[:, 3 * width :] = dot_rows(branch, mixed).astype(LOW)
    if parts == 1:
        outs[0][...] = total_ref[...]
    else:
        rows = D // parts
        for ref, half, order in zip(outs, (0, 0, 1, 1), FOLD_ORDERS):
            for at, m in enumerate(order):
                source = pl.multiple_of((place_ref[0] ^ m) * rows, rows)
                ref[at * rows : (at + 1) * rows, :] = total_ref[
                    pl.ds(source, rows), half * D // 2 : (half + 1) * D // 2
                ]


def fold_kernel(*refs):
    for at in range(2):
        keep_ref, came_ref = refs[2 * at : 2 * at + 2]
        kept_ref, sent_ref = refs[4 + 2 * at : 6 + 2 * at]
        rows = kept_ref.shape[0] // 2
        for block in range(4):
            here = slice(block * rows, (block + 1) * rows)
            to = slice(block // 2 * rows, (block // 2 + 1) * rows)
            total = keep_ref[here, :].astype(WIDE) + came_ref[here, :].astype(WIDE)
            if block % 2 == 0:
                kept_ref[to, :] = total
            else:
                sent_ref[to, :] = total.astype(LOW)


def last_fold_kernel(*refs):
    kept_ref, sent_ref = refs[4:]
    for at in range(2):
        keep_ref, came_ref = refs[2 * at : 2 * at + 2]
        rows, width = kept_ref.shape[0], keep_ref.shape[1]
        cols = slice(at * width, (at + 1) * width)
        total = keep_ref[...] + came_ref[...].astype(WIDE)
        kept_ref[:, cols] = total[:rows]
        sent_ref[:, cols] = total[rows:].astype(LOW)


def input_kernel(
    heads,
    place_ref,
    pg_ref,
    w_ref,
    x_ref,
    gain_ref,
    table_ref,
    early_ref,
    keep_ref,
    send_ref,
    wide_ref,
):
    tensor_place = place_ref[1]
    width = heads * HEAD_DIM
    wide_ref[...] = dot_cols(pg_ref[...], w_ref[:, : 3 * width])
    values = x_ref[...].astype(WIDE)
    scale = lax.rsqrt(jnp.mean(values * values, axis=-1, keepdims=True) + EPS_NORM)
    gain_grad = jnp.sum(wide_ref[...] * values * scale, axis=0, keepdims=True)
    quarter = SEQ_LEN // 4
    for half, distance in enumerate((0, 2)):
        near = pl.multiple_of((tensor_place ^ distance) * quarter, quarter)
        far = pl.multiple_of((tensor_place ^ distance ^ 1) * quarter, quarter)
        block = pl.ds(half * quarter, quarter)
        keep_ref[block, :] = wide_ref[pl.ds(near, quarter), :]
        send_ref[block, :] = wide_ref[pl.ds(far, quarter), :].astype(LOW)
    small = early_ref[...]
    line = lax.broadcasted_iota(jnp.int32, (small.shape[0], 1), 0)
    small = jnp.where(line == 0, gain_grad, small)
    for h in range(heads):
        counts = jnp.concatenate(
            [table_ref[h : h + 1, :], jnp.zeros((1, D - table_ref.shape[1]), WIDE)], axis=1
        )
        small = jnp.where(line == 1 + tensor_place * heads + h, counts, small)
    keep_ref[SEQ_LEN // 2 :, :] = small
    send_ref[SEQ_LEN // 2 :, :] = small.astype(LOW)


def update_kernel(*refs):
    came, weights, outs = refs[:-12], refs[-12:-6], refs[-6:]
    shard = weights[0].shape[1]
    total = jnp.zeros((shard, D), WIDE)
    for ref in came:
        for m in range(ref.shape[0] // shard):
            total = total + ref[m * shard : (m + 1) * shard, :].astype(WIDE)
    width = weights[0].shape[2]
    for c in range(3):
        grad = total[:, c * width : (c + 1) * width]
        made = adamw(*[ref[c] for ref in weights[:3]], grad, 3.0 * D ** (-0.5), DECAY)
        for ref, value in zip(outs[:3], made):
            ref[c] = value
    grad = jnp.transpose(total[:, 3 * width :])
    made = adamw(*[ref[...] for ref in weights[3:]], grad, 3.0 * FAN_O ** (-0.5), DECAY)
    for ref, value in zip(outs[3:], made):
        ref[...] = value


def gather_projections(own, ready, count):
    if count != 8:
        return [lax.all_gather(own, "expert", axis=0, tiled=True)], ready
    pieces = [own] + [None] * (count - 1)
    for m in range(count - 2, 0, -2):
        pieces[m] = swap(own, "expert", m)
    pieces[1] = swap(own, "expert", 1)
    pieces[2], ready = tie(pieces[2], ready)
    for m in range(2, count, 2):
        pieces[m + 1] = swap(pieces[m], "expert", 1)
    return pieces, ready


def body(
    block_input,
    cotangent,
    lengths,
    routes,
    norm_gains,
    gains_mean,
    gains_square,
    position_bias,
    bias_mean,
    bias_square,
    router,
    router_mean,
    router_square,
    qkv_weight,
    qkv_mean,
    qkv_square,
    out_weight,
    out_mean,
    out_square,
    expert_up,
    up_mean,
    up_square,
    expert_down,
    down_mean,
    down_square,
):
    tensor_size = lax.axis_size("tensor")
    tensor_place = lax.axis_index("tensor")
    expert_size = lax.axis_size("expert")
    place = lax.axis_index("expert")
    experts = expert_size // GROUP
    capacity = max(2, 9 * SEQ_LEN // (8 * expert_size))
    share = -(-capacity // tensor_size)
    own_slots = expert_size * share
    fan_down = max(1, FF // (experts * experts))
    heads_here = HEADS // tensor_size
    width = heads_here * HEAD_DIM
    rows_here = SEQ_LEN // tensor_size
    parts = expert_size if expert_size == 8 else 1
    shard = D // expert_size
    padded = -(-share // 8) * 8
    lines = -(-(2 + HEADS + experts) // 16) * 16
    scalars = jnp.stack([place, tensor_place]).astype(jnp.int32)

    own_shard = call(
        shard_kernel,
        [shape_of(LOW, shard, D)],
        [qkv_weight, out_weight],
        1,
        away=(0, 1),
        scratch=[
            pltpu.VMEM(qkv_weight.shape, WIDE),
            pltpu.VMEM(out_weight.shape, WIDE),
            pltpu.SemaphoreType.DMA((2,)),
        ],
    )[0]

    spread = np.zeros((expert_size, share, expert_size, padded), np.float32)
    for e in range(expert_size):
        spread[e, np.arange(share), e, np.arange(share)] = 1.0
    spread = jnp.asarray(spread.reshape(own_slots, expert_size * padded), LOW)
    offsets = np.arange(2 * SEQ_LEN)
    circular = np.where(offsets < SEQ_LEN, offsets, offsets - 2 * SEQ_LEN)
    circular_hits = jnp.asarray(offset_hits(circular, BUCKETS).T)
    half = expert_up.shape[1:]
    prepared = call(
        functools.partial(prepare_kernel, share),
        [
            shape_of(LOW, SEQ_LEN, D),
            shape_of(WIDE, heads_here, 2 * SEQ_LEN),
            shape_of(jnp.int32, 1, SEQ_LEN),
            shape_of(LOW, own_slots, D),
            shape_of(LOW, own_slots, D),
            shape_of(LOW, expert_size * padded, D),
            shape_of(LOW, *half),
            shape_of(LOW, *half),
        ],
        [
            scalars,
            routes.reshape(1, SEQ_LEN),
            norm_gains[0:1],
            spread,
            position_bias,
            circular_hits,
            block_input,
            cotangent,
            expert_up,
            expert_down,
        ],
        4,
        scalars=1,
        away=(6, 7, 8, 9),
        away_outs=(4, 6, 7),
        scratch=[
            pltpu.VMEM((SEQ_LEN, D), LOW),
            pltpu.VMEM((SEQ_LEN, D), LOW),
            pltpu.VMEM(expert_up.shape, WIDE),
            pltpu.VMEM(expert_up.shape, WIDE),
            pltpu.VMEM((own_slots, D), LOW),
            pltpu.VMEM(half, LOW),
            pltpu.VMEM(half, LOW),
            pltpu.SemaphoreType.DMA((7,)),
        ],
    )
    with jax.named_scope("cot_dispatch"):
        cot_came = exchange(prepared[5])
    prepared = prepared[:5] + prepared[6:]
    with jax.named_scope("projection_gather"):
        pieces, prepared = gather_projections(own_shard, prepared, expert_size)
    normed_one, offset_bias, slot_row, own_inputs, own_upstream, up_low, down_low = prepared
    joined = [shape_of(LOW, own_slots, D)]
    if parts > 1:
        down_low, pieces[6] = tie(down_low, pieces[6])
    with jax.named_scope("expert_gather"):
        down_far = swap(down_low, "expert", 2)
    projections, out_here = call(
        functools.partial(assemble_kernel, parts),
        [shape_of(LOW, D, D), shape_of(LOW, width, D)],
        [scalars] + pieces,
        1,
        scalars=1,
        scratch=[pltpu.SemaphoreType.DMA((parts,))],
        away=range(1, 1 + parts),
    )
    up_low, out_here = tie(up_low, out_here)
    with jax.named_scope("expert_gather"):
        up_near = swap(up_low, "expert", 1)
    with jax.named_scope("out_blocks"):
        out_blocks = tensor_blocks(out_here)
    projected, probs, *mixed_blocks = call(
        forward_kernel,
        [
            shape_of(LOW, SEQ_LEN, 3 * width),
            shape_of(LOW, heads_here, SEQ_LEN, SEQ_LEN),
        ]
        + [shape_of(LOW, own_slots, width)] * 4,
        [lengths, normed_one, offset_bias, slot_row, projections],
        6,
        scalars=1,
        away_outs=(0, 1),
        scratch=[
            pltpu.VMEM((SEQ_LEN, 3 * width), LOW),
            pltpu.VMEM((heads_here, SEQ_LEN, SEQ_LEN), LOW),
            pltpu.SemaphoreType.DMA((1 + heads_here,)),
        ],
    )
    router_rows = router.T

    mixed_blocks, up_near, down_far, cot_came = tie(mixed_blocks, up_near, down_far, cot_came)
    with jax.named_scope("expert_gather"):
        up_far = swap(jnp.concatenate([up_low, up_near], 0), "expert", 2)
        down_near = swap(jnp.concatenate([down_low, down_far], 0), "expert", 1)
    ups, downs = [up_low, up_near, up_far], [down_low, down_far, down_near]
    with jax.named_scope("mixed"):
        mixed_own = [mixed_blocks[0]] + [swap(mixed_blocks[m], "tensor", m) for m in range(1, 4)]
    own_cot = call(join_kernel, joined, [spread, cot_came], 1, limit=LIMIT_SMALL)[0]
    with jax.named_scope("cot_blocks"):
        grad_blocks = tensor_blocks(own_cot)

    middle, normed_two, rows_sent = call(
        middle_kernel,
        [
            shape_of(WIDE, own_slots, D),
            shape_of(LOW, own_slots, D),
            shape_of(LOW, expert_size * padded, D),
        ],
        [own_inputs, norm_gains[1:2], spread] + mixed_own + out_blocks,
        1,
    )
    with jax.named_scope("row_dispatch"):
        rows_came = exchange(rows_sent)
    own_rows = call(join_kernel, joined, [spread, rows_came], 1, limit=LIMIT_SMALL)[0]
    with jax.named_scope("row_blocks"):
        row_blocks = tensor_blocks(own_rows)

    hidden = 4 * expert_up.shape[1]
    rows_in, grad_rows, act, grad_pre, keep, send = call(
        expert_kernel,
        [
            shape_of(LOW, 4 * own_slots, D),
            shape_of(LOW, 4 * own_slots, D),
            shape_of(LOW, 4 * own_slots, hidden),
            shape_of(LOW, 4 * own_slots, hidden),
            shape_of(WIDE, 2 * own_slots, 2 * D),
            shape_of(LOW, 2 * own_slots, 2 * D),
        ],
        [scalars, router_rows] + row_blocks + grad_blocks + ups + downs,
        8,
        scalars=1,
        limit=LIMIT_SMALL,
    )
    half_up = shape_of(WIDE, hidden // 2, D)
    sent_up = shape_of(LOW, hidden // 2, D)
    up_keep, up_send, down_keep, down_send = call(
        expert_weights_kernel,
        [half_up, sent_up, half_up, sent_up],
        [rows_in, grad_rows, act, grad_pre],
        3,
        limit=LIMIT_SMALL,
    )
    with jax.named_scope("return_sum"):
        came = swap(send, "tensor", 1)
    came, up_send, down_send = tie(came, up_send, down_send)
    with jax.named_scope("expert_reduce"):
        up_came = swap(up_send, "expert", 2)
        down_came = swap(down_send, "expert", 1)
    kept, send = call(
        half_kernel,
        [shape_of(WIDE, own_slots, 2 * D), shape_of(LOW, own_slots, 2 * D)],
        [keep, came],
        1,
        limit=LIMIT_SMALL,
    )
    with jax.named_scope("return_sum"):
        came = swap(send, "tensor", 2)
    sent = call(
        spread_kernel,
        [shape_of(LOW, expert_size * padded, 2 * D)],
        [kept, came, spread],
        1,
        limit=LIMIT_SMALL,
    )[0]
    sent, up_came, down_came = tie(sent, up_came, down_came)
    with jax.named_scope("row_return"):
        returned = exchange(sent)
    quarter = (hidden // 4, D)
    up_half, up_send, down_half, down_send = call(
        reduce_kernel,
        [shape_of(WIDE, *quarter), shape_of(LOW, *quarter)] * 2,
        [up_keep, up_came, down_keep, down_came],
        1,
        limit=LIMIT_SMALL,
    )
    with jax.named_scope("expert_reduce"):
        up_last = swap(up_send, "expert", 1)
        down_last = swap(down_send, "expert", 2)

    branch_grad, block_slots, early, *mixed_grads = call(
        functools.partial(after_kernel, share),
        [
            shape_of(LOW, own_slots, D),
            shape_of(LOW, own_slots, D),
            shape_of(WIDE, lines, D),
        ]
        + [shape_of(LOW, own_slots, width)] * 4,
        [middle, normed_two, own_upstream, norm_gains[1:2], router_rows, spread, returned]
        + out_blocks,
        4,
    )
    with jax.named_scope("mixed_grad"):
        mixed_grads = [mixed_grads[0]] + [swap(mixed_grads[m], "tensor", m) for m in range(1, 4)]
    mixed_grads, branch_grad, up_last, down_last = tie(
        mixed_grads, branch_grad, up_last, down_last
    )
    with jax.named_scope("branch_blocks"):
        branch_far = swap(branch_grad, "tensor", 2)
        branch_near = swap(branch_grad, "tensor", 1)
    mirrored = np.arange(2 * SEQ_LEN) - (SEQ_LEN - 1)
    projected_grad, table_grad, _ = call(
        backward_kernel,
        [
            shape_of(LOW, SEQ_LEN, 3 * width),
            shape_of(WIDE, 8, 128),
            shape_of(WIDE, 8, 2 * SEQ_LEN),
        ],
        [slot_row, projected, probs, jnp.asarray(offset_hits(mirrored, 128))] + mixed_grads,
        5,
    )
    branch_far, projected_grad = tie(branch_far, projected_grad)
    with jax.named_scope("branch_blocks"):
        branch_both = swap(branch_far, "tensor", 1)
    branch_blocks = [branch_grad, branch_near, branch_far, branch_both]
    grad_sent = call(
        functools.partial(weights_kernel, parts),
        [shape_of(LOW, D, D)] if parts == 1 else [shape_of(LOW, D // 2, D // 2)] * 4,
        [scalars, normed_one, projected_grad] + list(mixed_blocks) + branch_blocks,
        2,
        limit=LIMIT_SMALL,
        scalars=1,
        scratch=[pltpu.VMEM((D, D), LOW)],
    )
    grad_sent, projected_grad = tie(grad_sent, projected_grad)
    with jax.named_scope("projection_reduce"):
        if parts == 1:
            grad_came = [exchange(grad_sent[0])]
        else:
            one_keep, one_sent, two_keep, two_sent = grad_sent
            one_came, two_came = swap(one_sent, "expert", 1), swap(two_sent, "expert", 2)
    keep, send = call(
        functools.partial(input_kernel, heads_here),
        [
            shape_of(WIDE, 2 * rows_here + lines, D),
            shape_of(LOW, 2 * rows_here + lines, D),
        ],
        [
            scalars,
            projected_grad,
            projections,
            block_input,
            norm_gains[0:1],
            table_grad,
            early,
        ],
        2,
        limit=LIMIT_SMALL,
        scalars=1,
        scratch=[pltpu.VMEM((SEQ_LEN, D), WIDE)],
    )
    with jax.named_scope("input_sum"):
        came = swap(send, "tensor", 1)
    came, up_half, down_half = tie(came, up_half, down_half)
    kept, send, middle_own = call(
        input_half_kernel,
        [
            shape_of(WIDE, rows_here + lines, D),
            shape_of(LOW, rows_here + lines, D),
            shape_of(WIDE, rows_here, D),
        ],
        [scalars, keep, came, slot_row] + branch_blocks,
        1,
        scalars=1,
        limit=LIMIT_SMALL,
    )
    state = pltpu.VMEM(expert_up.shape, WIDE)
    (
        new_up_mean,
        new_up_square,
        new_expert_up,
        new_down_mean,
        new_down_square,
        new_expert_down,
    ) = call(
        functools.partial(
            expert_update_kernel, (3.0 * D ** (-0.5), 3.0 * fan_down ** (-0.5))
        ),
        [shape_of(WIDE, *expert_up.shape)] * 6,
        [
            up_half,
            up_last,
            down_half,
            down_last,
            expert_up,
            up_mean,
            up_square,
            expert_down,
            down_mean,
            down_square,
        ],
        4,
        away=range(4, 10),
        away_outs=range(6),
        scratch=[state] * 12 + [pltpu.SemaphoreType.DMA((12,))],
    )
    if parts > 1:
        one_came, send, new_up_mean = tie(one_came, send, new_up_mean)
    with jax.named_scope("projection_reduce"):
        if parts > 1:
            one_came, block_slots = tie(one_came, block_slots)
            one_keep, one_sent, two_keep, two_sent = call(
                fold_kernel,
                [shape_of(WIDE, D // 4, D // 2), shape_of(LOW, D // 4, D // 2)] * 2,
                [one_keep, one_came, two_keep, two_came],
                1,
                limit=LIMIT_SMALL,
            )
            one_came, two_came = swap(one_sent, "expert", 2), swap(two_sent, "expert", 1)
            grad_kept, sent = call(
                last_fold_kernel,
                [shape_of(WIDE, shard, D), shape_of(LOW, shard, D)],
                [one_keep, one_came, two_keep, two_came],
                1,
                limit=LIMIT_SMALL,
            )
            grad_came = [grad_kept, swap(sent, "expert", 4)]
    with jax.named_scope("input_sum"):
        came = swap(send, "tensor", 2)
        small = kept[rows_here:] + came[rows_here:].astype(WIDE)
        grad_came, came = tie(grad_came, came)
        normed_one_grad = kept[:rows_here] + came[:rows_here].astype(WIDE)
    with jax.named_scope("block_blocks"):
        block_blocks = tensor_blocks(block_slots)

    with jax.named_scope("small_sum"):
        small = exchange(jnp.tile(small.astype(LOW), (expert_size, 1))).astype(WIDE)
        small = jnp.sum(small.reshape(expert_size, lines, D), axis=0)
    own_start = tensor_place * rows_here
    slot_own = lax.dynamic_slice_in_dim(slot_row[0], own_start, rows_here, 0)
    own_hits = (
        slot_own[:, None] == jnp.arange(tensor_size * own_slots, dtype=jnp.int32)[None, :]
    ).astype(LOW)
    block_output = dot_plain(own_hits, jnp.concatenate(block_blocks, 0)).astype(LOW)
    inputs_own = lax.dynamic_slice_in_dim(block_input, own_start, rows_here, 0).astype(WIDE)
    scale_own = lax.rsqrt(jnp.mean(inputs_own * inputs_own, axis=-1, keepdims=True) + EPS_NORM)
    weighted = normed_one_grad * norm_gains[0]
    inner = jnp.mean(weighted * inputs_own, axis=-1, keepdims=True)
    input_grad = (
        middle_own
        + scale_own * weighted
        - inputs_own * scale_own * scale_own * scale_own * inner
    )

    gains_grad = jnp.concatenate([small[0:1], small[1 + HEADS : 2 + HEADS]], 0)
    bias_grad = small[1 : 1 + HEADS, :BUCKETS].T
    router_grad = small[2 + HEADS : 2 + HEADS + experts].T

    new_gains_mean, new_gains_square, new_norm_gains = adamw(
        norm_gains, gains_mean, gains_square, gains_grad, 0.3, 0.0
    )
    new_bias_mean, new_bias_square, new_position_bias = adamw(
        position_bias, bias_mean, bias_square, bias_grad, 1.5, 0.0
    )
    new_router_mean, new_router_square, new_router = adamw(
        router, router_mean, router_square, router_grad, 3.0 * (2 * D) ** (-0.5), DECAY
    )
    new_qkv_mean, new_qkv_square, new_qkv_weight, new_out_mean, new_out_square, new_out_weight = (
        call(
            update_kernel,
            [shape_of(WIDE, *qkv_weight.shape)] * 3 + [shape_of(WIDE, *out_weight.shape)] * 3,
            grad_came
            + [
                qkv_weight,
                qkv_mean,
                qkv_square,
                out_weight,
                out_mean,
                out_square,
            ],
            40,
            )
    )
    return (
        block_output,
        input_grad,
        new_gains_mean,
        new_gains_square,
        new_norm_gains,
        new_bias_mean,
        new_bias_square,
        new_position_bias,
        new_router_mean,
        new_router_square,
        new_router,
        new_qkv_mean,
        new_qkv_square,
        new_qkv_weight,
        new_out_mean,
        new_out_square,
        new_out_weight,
        new_up_mean,
        new_up_square,
        new_expert_up,
        new_down_mean,
        new_down_square,
        new_expert_down,
    )


def solution(mesh):
    return jax.shard_map(
        body,
        mesh=mesh,
        in_specs=(
            P("expert", None),
            P("expert", None),
            P("expert"),
            P("expert", None),
            P(),
            P(),
            P(),
            P(),
            P(),
            P(),
            P(),
            P(),
            P(),
            P(None, "expert", "tensor"),
            P(None, "expert", "tensor"),
            P(None, "expert", "tensor"),
            P("tensor", "expert"),
            P("tensor", "expert"),
            P("tensor", "expert"),
            P("expert", "tensor", None),
            P("expert", "tensor", None),
            P("expert", "tensor", None),
            P("expert", "tensor", None),
            P("expert", "tensor", None),
            P("expert", "tensor", None),
        ),
        out_specs=(
            P(("expert", "tensor"), None),
            P(("expert", "tensor"), None),
            P(),
            P(),
            P(),
            P(),
            P(),
            P(),
            P(),
            P(),
            P(),
            P(None, "expert", "tensor"),
            P(None, "expert", "tensor"),
            P(None, "expert", "tensor"),
            P("tensor", "expert"),
            P("tensor", "expert"),
            P("tensor", "expert"),
            P("expert", "tensor", None),
            P("expert", "tensor", None),
            P("expert", "tensor", None),
            P("expert", "tensor", None),
            P("expert", "tensor", None),
            P("expert", "tensor", None),
        ),
        check_vma=False,
    )
```
